128 devices in a mesh: dp: 16 (over y, z_lo, core), expert: 8 (over z_hi, x).
Axes of the slice: x: 4, y: 4, z: 4 (z_hi: 2, z_lo: 2; z = z_hi * 2 + z_lo), core: 2. Of those that a mesh axis runs over, the one named last changes fastest.
Arguments:
- tokens: bfloat16 [32768, 768], P(('dp', 'expert')), may hold values from -6 to 6
- routes: int32 [32768, 2], P(('dp', 'expert')), may hold values from 0 to 7, all different within a row; in each aligned block of 256 rows (0 to 255, 256 to 511, ...) at most 128 rows name the same one
- lengths: int32 [128, 16], P(('dp', 'expert')), may hold values from 1 to 64, 256 in all within a row
- norm_gain: float32 [768], replicated, may hold values from 0.25 to 1.75
- router_weight: bfloat16 [768, 8], replicated, may hold values from -0.21875 to 0.21875
- gate_weight: bfloat16 [8, 768, 3072], P('expert'), may hold values from -0.21875 to 0.21875
- up_weight: bfloat16 [8, 768, 3072], P('expert'), may hold values from -0.21875 to 0.21875
- down_weight: bfloat16 [8, 3072, 768], P('expert'), may hold values from -0.109375 to 0.109375
Outputs:
- hidden_out: bfloat16 [32768, 768], P(('dp', 'expert'))
- query_grad: float32 [1024, 768], P(('dp', 'expert'))
- doc_grad: float32 [1024, 768], P(('dp', 'expert'))
The draws below stay inside these ranges and needn't reach their ends.
Inputs may be any that keep to these rules, and one draw needn't show every extreme that they name: `routes`: among the rows of one device no expert is named by more than 128 rows, a bound that some block reaches. `lengths`: each row sums to 256; the first 8 entries are queries, the others their documents in the same order; the largest entry is 64.
All inputs are finite; a program needn't handle non-finite values.
Results may differ from the reference program's by a relative error of at most 0.0053.
Values may be sent and summed in bfloat16 or wider, within the bound.
No kernel may reach another device: no remote copies, remote signals or barrier semaphores. Data moves between devices by JAX's collectives and lax.ppermute only.
A program may use at most 128 MiB of HBM per device.

```python
import math
import jax
import jax.numpy as jnp
import numpy as np
from jax import lax

D = 768
FF = 3072
TOP = 2
EXPERTS = 8
TOK_DEV = 256
CAP = 128
PAIRS_DEV = 8
SEQ_DEV = 16
SEQ_MOST = 64
TOKENS = 32768
QUERIES = 1024
DEVICES = 128


def steps_of(rng, shape, split, smallest, top_value):
    level, own = 1.0, jax.random.fold_in(rng, 6)
    for axis_at, shards_of in split:
        heights = jnp.exp(jax.random.uniform(jax.random.fold_in(own, axis_at), (shards_of,), jnp.float32, smallest / len(split), top_value / len(split)))
        level = level * jnp.repeat(heights, shape[axis_at] // shards_of).reshape([-1 if axis == axis_at else 1 for axis in range(len(shape))])
    return level


def split_up(count, total, limit, skew):
    portions = [(1 << 20) // math.isqrt(standing ** skew) + 1 for standing in range(2, count + 1)]
    rest, given = total - limit - (count - 1), [1] * (count - 1)
    while rest > 0:
        movable = [i for i in range(count - 1) if given[i] < limit]
        mass, remaining = sum([portions[i] for i in movable]), rest
        for i in movable:
            addition = min(limit - given[i], max(1, remaining * portions[i] // mass), rest)
            given[i] = given[i] + addition
            rest = rest - addition
    return np.array([limit] + given)


def uneven(rng, count, total, bound, lean):
    if count == 2:
        one = jax.random.randint(rng, (), max(1, total - bound), min(bound, total - 1) + 1)
        return jnp.stack([one, total - one])
    sizes = jnp.asarray(split_up(count, total, bound, lean), jnp.int32)
    couples = (count - 1) // 2
    giver, sink = sizes[1:1 + 2 * couples:2], sizes[2:2 + 2 * couples:2]
    room = jnp.minimum(giver - 1, bound - sink)
    passed = jax.random.randint(jax.random.fold_in(rng, 1), (couples,), 0, 1 << 20) % (room + 1)
    sizes = sizes.at[1:1 + 2 * couples:2].set(giver - passed).at[2:2 + 2 * couples:2].set(sink + passed)
    return sizes[jax.random.permutation(jax.random.fold_in(rng, 2), count)]


def routed_block(key, own, number, rows, amount, top, limit, slope):
    sequence = jax.random.permutation(key, amount)
    packed, ordinary = portions_of(amount, rows * top, limit, slope, True), portions_of(amount, rows * top, limit, slope, False)
    places = jnp.arange(amount)

    def named(sizes, turn):
        used = int((sizes > 0).sum())
        fixed = max(1, used // 4)
        moved = fixed + (places - fixed + turn * (used - fixed)) % max(1, amount - fixed)
        return jnp.zeros((amount,), jnp.int32).at[sequence[jnp.where(places < fixed, places, moved)]].set(jnp.asarray(sizes, jnp.int32))

    sizes = jnp.where(number % 4 == 0, named(packed, number // 4), named(ordinary, number - number // 4 - 1))
    mixed = jax.random.permutation(jax.random.fold_in(own, 3), amount)
    giver, taker = mixed[0:amount // 2 * 2:2], mixed[1:amount // 2 * 2:2]
    margin = jnp.minimum(sizes[giver] - 1, limit - sizes[taker]) // 2
    margin = jnp.where((giver == sequence[0]) | (taker == sequence[0]) | (sizes[taker] == 0), 0, jnp.maximum(margin, 0))
    moved = jax.random.randint(jax.random.fold_in(own, 4), (amount // 2,), 0, 1 << 20) % (margin + 1)
    sizes = sizes.at[giver].add(-moved).at[taker].add(moved)
    items = jnp.searchsorted(jnp.cumsum(sizes), jnp.arange(rows * top), side="right").astype(jnp.int32)
    listing = items.reshape(top, rows).T
    listing = listing[jax.random.permutation(jax.random.fold_in(own, 1), rows)]
    turn = jax.random.randint(jax.random.fold_in(own, 2), (rows, 1), 0, top)
    return jnp.take_along_axis(listing, (jnp.arange(top)[None, :] + turn) % top, axis=1)


def portions_of(amount, total, bound, skew, full):
    portions = [(1 << 20) // math.isqrt(grade ** skew) + 1 for grade in range(1, amount + 1)]
    largest = bound if full else min(bound, max(-(-total // amount), total * portions[0] // sum(portions)))
    least = 1 if total - largest >= amount - 1 else 0
    holding, surplus = [largest] + [least] * (amount - 1), total - largest - least * (amount - 1)
    while surplus > 0:
        free = [i for i in range(1, amount) if holding[i] < largest] or [i for i in range(1, amount) if holding[i] < bound]
        whole, left = sum([portions[i] for i in free]), surplus
        for i in free:
            addition = min(bound - holding[i], max(1, left * portions[i] // whole), surplus)
            holding[i] = holding[i] + addition
            surplus = surplus - addition
    return np.array(holding)


def gaussian(own_key, dims, spread, bound, pieces=(), kind=jnp.bfloat16):
    result = jax.random.normal(own_key, dims, jnp.float32) * spread
    if len(pieces) > 0:
        result = steps_of(own_key, dims, pieces, -0.22, 0.18) * result
    return jnp.clip(result, min=-bound, max=bound).astype(kind)


def setup_inputs(seed: int = 0) -> dict:
    key_list = jax.random.split(jax.random.key(seed), 9)
    tokens = gaussian(key_list[0], (TOKENS, D), 1.0, 6.0, ((0, 128),))
    routes_keys = jax.random.split(jax.random.fold_in(key_list[1], 1), TOKENS // TOK_DEV)
    routes_turns = jax.random.permutation(jax.random.fold_in(key_list[1], 3), TOKENS // TOK_DEV)
    routes = jax.vmap(lambda own, number: routed_block(jax.random.fold_in(key_list[1], 2), own, number, TOK_DEV, EXPERTS, TOP, CAP, 2))(routes_keys, routes_turns).reshape((TOKENS, TOP))
    lengths = jax.vmap(lambda own: uneven(own, SEQ_DEV, TOK_DEV, SEQ_MOST, 2))(jax.random.split(key_list[2], DEVICES)).reshape((DEVICES, SEQ_DEV)).astype(jnp.int32)
    norm_gain = jnp.clip(1.0 + 0.15 * jax.random.normal(key_list[3], (D,), jnp.float32), 0.25, 1.75)
    router_weight = gaussian(key_list[4], (D, EXPERTS), D ** -0.5, 0.21875)
    gate_weight = gaussian(key_list[5], (EXPERTS, D, FF), D ** -0.5, 0.21875, ((0, 8),))
    up_weight = gaussian(key_list[6], (EXPERTS, D, FF), D ** -0.5, 0.21875, ((0, 8),))
    down_weight = gaussian(key_list[7], (EXPERTS, FF, D), FF ** -0.5, 0.109375, ((0, 8),))
    return dict(tokens=tokens, routes=routes, lengths=lengths, norm_gain=norm_gain, router_weight=router_weight, gate_weight=gate_weight, up_weight=up_weight, down_weight=down_weight)


logit_scale = 50.0
norm_eps = 1e-06
pool_eps = 1e-06

def rms_normalize(tokens, norm_gain):
    widened = tokens.astype(jnp.float32)
    inverse = lax.rsqrt(lax.optimization_barrier(jnp.mean(widened * widened, axis=-1, keepdims=True)) + norm_eps)
    return (widened * inverse * norm_gain).astype(jnp.bfloat16)

def pair_weights(normed, router_weight, routes):
    logits = jnp.dot(normed, router_weight, preferred_element_type=jnp.float32)
    labels = jnp.arange(router_weight.shape[1], dtype=jnp.int32)
    chosen = lax.optimization_barrier(jnp.sum(jnp.where(routes[:, :, None] == labels[None, None, :], logits[:, None, :], 0.0), axis=-1))
    leading = jax.nn.sigmoid(chosen[:, 0] - chosen[:, 1])
    return jnp.stack([leading, 1.0 - leading], axis=1)

def expert_rows(row_block, w_gate, w_up, w_down):
    gate_act = jnp.dot(row_block, w_gate, preferred_element_type=jnp.float32)
    up_act = jnp.dot(row_block, w_up, preferred_element_type=jnp.float32)
    hidden = (jax.nn.silu(gate_act) * up_act).astype(jnp.bfloat16)
    return jnp.dot(hidden, w_down, preferred_element_type=jnp.float32).astype(jnp.bfloat16)

def embed(mixed, lengths):
    starts = jnp.cumsum(lengths, axis=1, dtype=jnp.int32) - lengths
    places = jnp.arange(mixed.shape[1], dtype=jnp.int32)
    member = ((places[None, None, :] >= starts[:, :, None]) & (places[None, None, :] < (starts + lengths)[:, :, None])).astype(jnp.float32)
    pooled = jnp.einsum('gst,gtd->gsd', member, mixed, precision=lax.Precision.HIGHEST) / lengths[:, :, None].astype(jnp.float32)
    return pooled * lax.rsqrt(lax.optimization_barrier(jnp.sum(pooled * pooled, axis=-1, keepdims=True)) + pool_eps)

def reference(tokens, routes, lengths, norm_gain, router_weight, gate_weight, up_weight, down_weight):
    normed = rms_normalize(tokens, norm_gain)
    route_weights = pair_weights(normed, router_weight, routes)
    expert_ids = routes.reshape(-1)
    token_ids = jnp.arange(TOKENS * TOP, dtype=jnp.int32) // TOP
    onehot = (expert_ids[:, None] == jnp.arange(EXPERTS, dtype=jnp.int32)[None, :]).astype(jnp.int32)
    ranking = lax.optimization_barrier(jnp.sum((jnp.cumsum(onehot, axis=0, dtype=jnp.int32) - onehot) * onehot, axis=1, dtype=jnp.int32))
    counts = lax.optimization_barrier(jnp.sum(onehot, axis=0, dtype=jnp.int32))
    padded = (counts + 127) // 128 * 128
    starts = jnp.cumsum(padded, dtype=jnp.int32) - padded
    position = lax.optimization_barrier(jnp.sum(onehot * starts[None, :], axis=1, dtype=jnp.int32)) + ranking
    block_count = (TOKENS * TOP + 127) // 128 + EXPERTS
    sectioned = jnp.zeros((block_count * 128, D), jnp.bfloat16).at[position].set(normed[token_ids])
    ends = starts + padded
    block_start = jnp.arange(block_count, dtype=jnp.int32) * 128
    owner = jnp.minimum(lax.optimization_barrier(jnp.sum((block_start[:, None] >= ends[None, :]).astype(jnp.int32), axis=1, dtype=jnp.int32)), EXPERTS - 1)

    def run_block(item):
        row_block, expert = item
        return expert_rows(row_block, gate_weight[expert], up_weight[expert], down_weight[expert])
    served = lax.map(run_block, (sectioned.reshape(block_count, 128, D), owner)).reshape(block_count * 128, D)
    returned = served[position].reshape(TOKENS, TOP, D).astype(jnp.float32)
    mixed = tokens.astype(jnp.float32) + lax.optimization_barrier(jnp.sum(route_weights[:, :, None] * returned, axis=1))
    hidden_out = mixed.astype(jnp.bfloat16)
    embedded = embed(mixed.reshape(DEVICES, TOK_DEV, D), lengths)
    queries = embedded[:, :PAIRS_DEV].reshape(QUERIES, D)
    documents = embedded[:, PAIRS_DEV:].reshape(QUERIES, D)
    scores = logit_scale * jnp.dot(queries, documents.T, precision=lax.Precision.HIGHEST)
    exps = jnp.exp(scores)
    likely = exps / lax.optimization_barrier(jnp.sum(exps, axis=-1, keepdims=True))
    coefficient = logit_scale * (likely - jnp.eye(QUERIES, dtype=jnp.float32))
    query_grad = jnp.dot(coefficient, documents, precision=lax.Precision.HIGHEST)
    doc_grad = jnp.dot(coefficient.T, queries, precision=lax.Precision.HIGHEST)
    return (hidden_out, query_grad, doc_grad)
```

```python
import jax
import jax.numpy as jnp
from jax import lax
from jax.sharding import PartitionSpec as P

logit_scale = 50.0
norm_eps = 1e-06
pool_eps = 1e-06


def rms_normalize(tokens, norm_gain):
    widened = tokens.astype(jnp.float32)
    inverse = lax.rsqrt(jnp.mean(widened * widened, axis=-1, keepdims=True) + norm_eps)
    return (widened * inverse * norm_gain).astype(jnp.bfloat16)


def expert_rows(row_block, w_gate, w_up, w_down):
    gate_act = jnp.dot(row_block, w_gate, preferred_element_type=jnp.float32)
    up_act = jnp.dot(row_block, w_up, preferred_element_type=jnp.float32)
    hidden = (jax.nn.silu(gate_act) * up_act).astype(jnp.bfloat16)
    return jnp.dot(hidden, w_down, preferred_element_type=jnp.float32).astype(jnp.bfloat16)


def embed(mixed, lengths):
    starts = jnp.cumsum(lengths, axis=1, dtype=jnp.int32) - lengths
    places = jnp.arange(mixed.shape[1], dtype=jnp.int32)
    member = (
        (places[None, None, :] >= starts[:, :, None])
        & (places[None, None, :] < (starts + lengths)[:, :, None])
    ).astype(jnp.float32)
    pooled = jnp.einsum("gst,gtd->gsd", member, mixed, precision=lax.Precision.HIGHEST) / lengths[
        :, :, None
    ].astype(jnp.float32)
    return pooled * lax.rsqrt(jnp.sum(pooled * pooled, axis=-1, keepdims=True) + pool_eps)


def dot_nt(a, b):
    return lax.dot_general(a, b, (((1,), (1,)), ((), ())), preferred_element_type=jnp.float32)


def halves(x):
    high = x.astype(jnp.bfloat16)
    return jnp.concatenate([high, (x - high.astype(jnp.float32)).astype(jnp.bfloat16)])


def fold(x):
    return x[: x.shape[0] // 2] + x[x.shape[0] // 2 :]


def gradients(queries, documents, all_queries, all_docs, member):
    count = queries.shape[0]
    total = all_docs.shape[0]
    sums = jnp.sum(jnp.exp(logit_scale * dot_nt(all_docs, all_queries)), axis=0, keepdims=True)
    columns = jnp.arange(total, dtype=jnp.int32)[None, :]
    own = columns == (member * count + jnp.arange(count, dtype=jnp.int32))[:, None]
    pair = jnp.exp(logit_scale * jnp.sum(queries * documents, axis=-1, keepdims=True))
    rows = jnp.where(own, 0.0, jnp.exp(logit_scale * fold(dot_nt(halves(queries), all_docs))))
    row_sum = jnp.sum(rows, axis=-1, keepdims=True) + pair
    diagonal = pair / row_sum - 1.0
    rest = fold(jnp.dot(halves(rows / row_sum), all_docs, preferred_element_type=jnp.float32))
    query_grad = logit_scale * (rest + diagonal * documents)
    cols = jnp.where(own, 0.0, jnp.exp(logit_scale * fold(dot_nt(halves(documents), all_queries))))
    rest = fold(jnp.dot(halves(cols / sums), all_queries, preferred_element_type=jnp.float32))
    doc_grad = logit_scale * (rest + diagonal * queries)
    return query_grad, doc_grad


def body(tokens, routes, lengths, norm_gain, router_weight, gate_weight, up_weight, down_weight):
    tok_rows, width = tokens.shape
    expert_count = router_weight.shape[1]
    capacity = tok_rows // 2
    normed = rms_normalize(tokens, norm_gain)
    logits = jnp.dot(normed, router_weight, preferred_element_type=jnp.float32)
    labels = jnp.arange(expert_count, dtype=jnp.int32)
    picked = routes[:, :, None] == labels[None, None, :]
    chosen = jnp.sum(jnp.where(picked, logits[:, None, :], 0.0), axis=-1)
    leading = jax.nn.sigmoid(chosen[:, 0] - chosen[:, 1])
    route_weights = jnp.stack([leading, 1.0 - leading], axis=1)
    flat_hits = picked.reshape(-1, expert_count).astype(jnp.int32)
    ranking = jnp.sum(
        (jnp.cumsum(flat_hits, axis=0, dtype=jnp.int32) - flat_hits) * flat_hits,
        axis=1,
        dtype=jnp.int32,
    )
    slot_ids = routes.reshape(-1) * capacity + ranking
    slot_grid = slot_ids.reshape(tok_rows, 2)
    spots = jnp.arange(expert_count * capacity, dtype=jnp.int32)
    dispatch = jnp.any(spots[:, None, None] == slot_grid[None, :, :], axis=-1).astype(jnp.bfloat16)
    outgoing = jnp.dot(dispatch, normed, preferred_element_type=jnp.float32).astype(jnp.bfloat16)
    outgoing = outgoing.reshape(expert_count, capacity, width)
    w_gate = gate_weight[0]
    w_up = up_weight[0]
    w_down = down_weight[0]
    incoming = lax.all_to_all(outgoing, "expert", split_axis=0, concat_axis=0, tiled=True)
    sources, slot_span, feature_count = incoming.shape
    results = expert_rows(
        incoming.reshape(sources * slot_span, feature_count), w_gate, w_up, w_down
    )
    results = results.reshape(sources, slot_span, feature_count)
    returned = lax.all_to_all(results, "expert", split_axis=0, concat_axis=0, tiled=True)
    back_rows = returned.reshape(expert_count * capacity, width)
    gathered_rows = back_rows[slot_ids].reshape(tok_rows, 2, width).astype(jnp.float32)
    mixed = tokens.astype(jnp.float32) + jnp.sum(route_weights[:, :, None] * gathered_rows, axis=1)
    hidden_out = mixed.astype(jnp.bfloat16)
    embedded = embed(mixed[None], lengths)[0]
    pair_count = embedded.shape[0] // 2
    queries = embedded[:pair_count]
    documents = embedded[pair_count:]

    groups = lax.axis_size("dp")
    devices = groups * expert_count
    same_core = [
        [d for d in range(devices) if (d // expert_count) % 2 == core] for core in range(2)
    ]
    chips = devices // 2
    copies = jnp.broadcast_to(embedded.astype(jnp.bfloat16)[None], (chips,) + embedded.shape)
    mine = lax.all_to_all(
        copies, ("dp", "expert"), split_axis=0, concat_axis=0, tiled=True, axis_index_groups=same_core
    )
    other = lax.ppermute(mine, "dp", [(i, i ^ 1) for i in range(groups)])
    both = jnp.concatenate([mine, other])
    all_queries = both[:, :pair_count].reshape(devices * pair_count, width)
    all_docs = both[:, pair_count:].reshape(devices * pair_count, width)
    member = lax.axis_index("dp") // 2 * expert_count + lax.axis_index("expert")
    query_grad, doc_grad = gradients(queries, documents, all_queries, all_docs, member)
    return (hidden_out, query_grad, doc_grad)


def solution(mesh):
    placed = (
        P(("dp", "expert"), None),
        P(("dp", "expert"), None),
        P(("dp", "expert"), None),
        P(),
        P(),
        P("expert", None, None),
        P("expert", None, None),
        P("expert", None, None),
    )
    return jax.shard_map(
        body,
        mesh=mesh,
        in_specs=placed,
        out_specs=(P(("dp", "expert"), None), P(("dp", "expert"), None), P(("dp", "expert"), None)),
        check_vma=False,
    )
```

```python
import functools

import jax
import jax.numpy as jnp
from jax import lax
from jax.experimental import pallas as pl
from jax.experimental.pallas import tpu as pltpu
from jax.sharding import PartitionSpec as P

logit_scale = 50.0
norm_eps = 1e-06
pool_eps = 1e-06
f32 = jnp.float32
bf16 = jnp.bfloat16
vmem_budget = 56 * 1024 * 1024


def dot(a, b):
    return jnp.dot(a, b, preferred_element_type=f32)


def dot_nt(a, b):
    return lax.dot_general(a, b, (((1,), (1,)), ((), ())), preferred_element_type=f32)


def iota(shape, axis):
    return lax.broadcasted_iota(jnp.int32, shape, axis)


def split(x):
    high = x.astype(bf16)
    return high, (x - high.astype(f32)).astype(bf16)


def fold(x):
    return x[: x.shape[0] // 2] + x[x.shape[0] // 2 :]


def call(kernel, outs, *operands, **options):
    return pl.pallas_call(
        kernel,
        out_shape=outs,
        compiler_params=pltpu.CompilerParams(vmem_limit_bytes=vmem_budget),
        **options,
    )(*operands)


def route_kernel(tokens_ref, routes_ref, gain_ref, router_ref, out_ref, slots_ref, weights_ref):
    rows = tokens_ref.shape[0]
    experts = router_ref.shape[0]
    capacity = out_ref.shape[0] // experts
    widened = tokens_ref[...].astype(f32)
    inverse = lax.rsqrt(jnp.mean(widened * widened, axis=-1, keepdims=True) + norm_eps)
    normed = (widened * inverse * gain_ref[...]).astype(bf16)
    labels = iota((experts, rows), 0)
    hit = (routes_ref[0:1, :] == labels) | (routes_ref[1:2, :] == labels)
    hits = jnp.where(hit, 1.0, 0.0).astype(bf16)
    down, across = iota((rows, rows), 0), iota((rows, rows), 1)
    ranks = dot(hits, jnp.where(down < across, 1.0, 0.0).astype(bf16))
    ranks = jnp.where(hit, ranks, -1.0)
    places = iota((capacity, rows), 0).astype(f32)
    for e in range(experts):
        chosen = jnp.where(places == ranks[e : e + 1, :], 1.0, 0.0).astype(bf16)
        out_ref[e * capacity : (e + 1) * capacity, :] = dot(chosen, normed).astype(bf16)
    hits_down = dot_nt(jnp.where(down == across, 1.0, 0.0).astype(bf16), hits)
    ranks_down = dot_nt(jnp.where(across < down, 1.0, 0.0).astype(bf16), hits)
    logits = dot_nt(normed, router_ref[...])
    both = jnp.sum(hits_down * logits, axis=-1, keepdims=True)
    slots_ref[...] = jnp.where(hits_down > 0.5, ranks_down, -1.0)
    weights_ref[...] = hits_down / (1.0 + jnp.exp(both - 2.0 * logits))


def expert_kernel(x_ref, gate_ref, up_ref, down_ref, out_ref, acc_ref, *, chunk):
    step, last = pl.program_id(0), pl.num_programs(0) - 1
    for at in range(0, x_ref.shape[0], chunk):
        rows = pl.ds(at, chunk)
        x = x_ref[rows, :]
        gate_act = dot(x, gate_ref[...])
        up_act = dot(x, up_ref[...])
        hidden = (gate_act / (1.0 + jnp.exp(-gate_act)) * up_act).astype(bf16)
        part = dot(hidden, down_ref[...])

        @pl.when(step == 0)
        def _():
            acc_ref[rows, :] = part

        @pl.when((step > 0) & (step < last))
        def _():
            acc_ref[rows, :] += part

        @pl.when(step == last)
        def _():
            out_ref[rows, :] = (acc_ref[rows, :] + part).astype(bf16)


def expert_rows(x, w_gate, w_up, w_down, block=512, chunk=1024):
    rows, width = x.shape
    hidden = w_gate.shape[1]
    whole = pl.BlockSpec((rows, width), lambda i: (0, 0))
    return pl.pallas_call(
        functools.partial(expert_kernel, chunk=chunk),
        out_shape=jax.ShapeDtypeStruct((rows, width), bf16),
        grid=(hidden // block,),
        in_specs=[
            whole,
            pl.BlockSpec((width, block), lambda i: (0, i)),
            pl.BlockSpec((width, block), lambda i: (0, i)),
            pl.BlockSpec((block, width), lambda i: (i, 0)),
        ],
        out_specs=whole,
        scratch_shapes=[pltpu.VMEM((rows, width), f32)],
        compiler_params=pltpu.CompilerParams(vmem_limit_bytes=vmem_budget),
    )(x, w_gate, w_up, w_down)


def combine_kernel(tokens_ref, slots_ref, weights_ref, back_ref, lengths_ref, hidden_ref, embedded_ref):
    rows = tokens_ref.shape[0]
    experts = slots_ref.shape[1]
    capacity = back_ref.shape[0] // experts
    lanes = iota((rows, capacity), 1).astype(f32)
    terms = [
        jnp.where(lanes == slots_ref[:, e : e + 1], weights_ref[:, e : e + 1], 0.0)
        for e in range(experts)
    ]
    high, low = split(jnp.concatenate(terms, axis=1))
    back = back_ref[...]
    mixed = tokens_ref[...].astype(f32) + (dot(high, back) + dot(low, back))
    hidden_ref[...] = mixed.astype(bf16)
    count = lengths_ref.shape[1]
    spans = jnp.broadcast_to(lengths_ref[...], (count, count)).astype(f32)
    down, across = iota((count, count), 0), iota((count, count), 1)
    ends = jnp.sum(jnp.where(across <= down, spans, 0.0), axis=1, keepdims=True)
    sizes = jnp.sum(jnp.where(across == down, spans, 0.0), axis=1, keepdims=True)
    places = iota((count, rows), 1).astype(f32)
    member = jnp.where((places >= ends - sizes) & (places < ends), 1.0, 0.0).astype(bf16)
    first, rest = split(mixed)
    second, third = split(mixed - first.astype(f32))
    pooled = (dot(member, first) + dot(member, second) + dot(member, third)) / sizes
    embedded_ref[...] = pooled * lax.rsqrt(
        jnp.sum(pooled * pooled, axis=-1, keepdims=True) + pool_eps
    )


def gradients(queries_ref, docs_ref, embedded_ref, first, query_grad_ref, doc_grad_ref):
    embedded = embedded_ref[...]
    count = embedded.shape[0] // 2
    total = queries_ref.shape[0]
    queries, documents = embedded[:count], embedded[count:]
    all_queries, all_docs = queries_ref[...], docs_ref[...]
    block = 256
    sums = jnp.zeros((1, total), f32)
    for at in range(0, total, block):
        scores = dot_nt(docs_ref[at : at + block, :], all_queries)
        sums = sums + jnp.sum(jnp.exp(logit_scale * scores), axis=0, keepdims=True)
    stacked = jnp.concatenate(split(embedded), axis=0)
    rows = fold(dot_nt(stacked, all_docs))[:count]
    cols = fold(dot_nt(stacked, all_queries))[count:]
    own = iota((count, total), 1) == first + iota((count, total), 0)
    pair = jnp.exp(logit_scale * jnp.sum(queries * documents, axis=-1, keepdims=True))
    rows = jnp.where(own, 0.0, jnp.exp(logit_scale * rows))
    cols = jnp.where(own, 0.0, jnp.exp(logit_scale * cols))
    row_sum = jnp.sum(rows, axis=-1, keepdims=True) + pair
    diagonal = pair / row_sum - 1.0
    likely = jnp.concatenate([rows / row_sum, cols / sums], axis=0)
    likely = jnp.concatenate(split(likely), axis=0)
    query_grad_ref[...] = logit_scale * (fold(dot(likely, all_docs))[:count] + diagonal * documents)
    doc_grad_ref[...] = logit_scale * (fold(dot(likely, all_queries))[count:] + diagonal * queries)


def gradient_kernel(place_ref, mine_ref, other_ref, embedded_ref, query_grad_ref, doc_grad_ref):
    core, first = place_ref[0], place_ref[1]

    @pl.when(core == 0)
    def _():
        gradients(mine_ref, other_ref, embedded_ref, first, query_grad_ref, doc_grad_ref)

    @pl.when(core == 1)
    def _():
        gradients(other_ref, mine_ref, embedded_ref, first, query_grad_ref, doc_grad_ref)


def route(tokens, routes, norm_gain, router_weight):
    rows, width = tokens.shape
    experts = router_weight.shape[1]
    return call(
        route_kernel,
        [
            jax.ShapeDtypeStruct((rows // 2 * experts, width), bf16),
            jax.ShapeDtypeStruct((rows, experts), f32),
            jax.ShapeDtypeStruct((rows, experts), f32),
        ],
        tokens, routes.T, norm_gain[None], router_weight.T,
    )


def combine(tokens, slots, weights, back, lengths):
    return call(
        combine_kernel,
        [
            jax.ShapeDtypeStruct(tokens.shape, bf16),
            jax.ShapeDtypeStruct((lengths.shape[1], tokens.shape[1]), f32),
        ],
        tokens, slots, weights, back, lengths,
    )


def info_nce(place, mine, other, embedded):
    out = jax.ShapeDtypeStruct((embedded.shape[0] // 2, embedded.shape[1]), f32)
    vmem = pl.BlockSpec(memory_space=pltpu.VMEM)
    return call(
        gradient_kernel, [out, out], place, mine, other, embedded,
        in_specs=[pl.BlockSpec(memory_space=pltpu.SMEM), vmem, vmem, vmem],
    )


def body(tokens, routes, lengths, norm_gain, router_weight, gate_weight, up_weight, down_weight):
    width = tokens.shape[1]
    experts = router_weight.shape[1]
    outgoing, slots, weights = route(tokens, routes, norm_gain, router_weight)
    outgoing = outgoing.reshape(experts, -1, width)
    incoming = lax.all_to_all(outgoing, "expert", split_axis=0, concat_axis=0, tiled=True)
    results = expert_rows(
        incoming.reshape(-1, width), gate_weight[0], up_weight[0], down_weight[0]
    )
    results = results.reshape(experts, -1, width)
    returned = lax.all_to_all(results, "expert", split_axis=0, concat_axis=0, tiled=True)
    hidden_out, embedded = combine(tokens, slots, weights, returned.reshape(-1, width), lengths)

    pairs = embedded.shape[0] // 2
    groups = lax.axis_size("dp")
    devices = groups * experts
    chips = devices // 2
    same_core = [[d for d in range(devices) if d // experts % 2 == core] for core in range(2)]
    swap = [(i, i ^ 1) for i in range(groups)]
    core = lax.axis_index("dp") % 2
    rounded = embedded.astype(bf16)
    kept = jnp.where(core == 0, rounded[:pairs], rounded[pairs:])
    given = jnp.where(core == 0, rounded[pairs:], rounded[:pairs])
    taken = lax.ppermute(given, "dp", swap)
    shard = jnp.concatenate(
        [jnp.where(core == 0, kept, taken), jnp.where(core == 0, taken, kept)]
    )
    copies = jnp.broadcast_to(shard[None], (chips,) + shard.shape)
    mine = lax.all_to_all(
        copies, ("dp", "expert"), split_axis=0, concat_axis=0, tiled=True, axis_index_groups=same_core
    ).reshape(-1, width)
    other = lax.ppermute(mine, "dp", swap)
    chip = lax.axis_index("dp") // 2 * experts + lax.axis_index("expert")
    place = jnp.stack([core, (chip * 2 + core) * pairs]).astype(jnp.int32)
    query_grad, doc_grad = info_nce(place, mine, other, embedded)
    return (hidden_out, query_grad, doc_grad)


def solution(mesh):
    placed = (
        P(("dp", "expert"), None),
        P(("dp", "expert"), None),
        P(("dp", "expert"), None),
        P(),
        P(),
        P("expert", None, None),
        P("expert", None, None),
        P("expert", None, None),
    )
    return jax.shard_map(
        body,
        mesh=mesh,
        in_specs=placed,
        out_specs=(P(("dp", "expert"), None), P(("dp", "expert"), None), P(("dp", "expert"), None)),
        check_vma=False,
    )
```

```python
import functools

import jax
import jax.numpy as jnp
from jax import lax
from jax.experimental import pallas as pl
from jax.experimental.pallas import tpu as pltpu
from jax.sharding import PartitionSpec as P

logit_scale = 50.0
norm_eps = 1e-06
pool_eps = 1e-06
f32 = jnp.float32
bf16 = jnp.bfloat16
mebibyte = 1024 * 1024


def dot(a, b):
    return jnp.dot(a, b, preferred_element_type=f32)


def dot_nt(a, b):
    return lax.dot_general(a, b, (((1,), (1,)), ((), ())), preferred_element_type=f32)


def iota(shape, axis):
    return lax.broadcasted_iota(jnp.int32, shape, axis)


def split(x):
    high = x.astype(bf16)
    return high, (x - high.astype(f32)).astype(bf16)


def fold(x):
    return x[: x.shape[0] // 2] + x[x.shape[0] // 2 :]


def call(kernel, outs, *operands, budget=16, **options):
    whole = pl.BlockSpec(memory_space=pltpu.VMEM)
    return pl.pallas_call(
        kernel,
        out_shape=outs,
        in_specs=[whole] * len(operands),
        out_specs=jax.tree.map(lambda _: whole, outs),
        compiler_params=pltpu.CompilerParams(vmem_limit_bytes=budget * mebibyte),
        **options,
    )(*operands)


def route_kernel(tokens_ref, routes_ref, gain_ref, router_ref, out_ref, slots_ref, weights_ref):
    rows = tokens_ref.shape[0]
    experts = router_ref.shape[0]
    capacity = out_ref.shape[0] // experts
    widened = tokens_ref[...].astype(f32)
    inverse = lax.rsqrt(jnp.mean(widened * widened, axis=-1, keepdims=True) + norm_eps)
    normed = (widened * inverse * gain_ref[...]).astype(bf16)
    labels = iota((experts, rows), 0)
    hit = (routes_ref[0:1, :] == labels) | (routes_ref[1:2, :] == labels)
    hits = jnp.where(hit, 1.0, 0.0).astype(bf16)
    down, across = iota((rows, rows), 0), iota((rows, rows), 1)
    ranks = dot(hits, jnp.where(down < across, 1.0, 0.0).astype(bf16))
    ranks = jnp.where(hit, ranks, -1.0)
    places = iota((capacity, rows), 0).astype(f32)
    for e in range(experts):
        chosen = jnp.where(places == ranks[e : e + 1, :], 1.0, 0.0).astype(bf16)
        out_ref[e * capacity : (e + 1) * capacity, :] = dot(chosen, normed).astype(bf16)
    hits_down = dot_nt(jnp.where(down == across, 1.0, 0.0).astype(bf16), hits)
    ranks_down = dot_nt(jnp.where(across < down, 1.0, 0.0).astype(bf16), hits)
    logits = dot_nt(normed, router_ref[...])
    both = jnp.sum(hits_down * logits, axis=-1, keepdims=True)
    slots_ref[...] = jnp.where(hits_down > 0.5, ranks_down, -1.0)
    weights_ref[...] = hits_down / (1.0 + jnp.exp(both - 2.0 * logits))


def expert_kernel(x_ref, gate_ref, up_ref, down_ref, out_ref, hidden_ref, *, block):
    def columns(step, carry):
        part = pl.ds(pl.multiple_of(step * block, block), block)
        x = x_ref[...]
        gate_act = dot(x, gate_ref[:, part])
        up_act = dot(x, up_ref[:, part])
        hidden_ref[:, part] = (gate_act / (1.0 + jnp.exp(-gate_act)) * up_act).astype(bf16)
        return carry

    lax.fori_loop(0, hidden_ref.shape[1] // block, columns, 0)
    out_ref[...] = dot(hidden_ref[...], down_ref[...]).astype(bf16)


def expert_rows(x, w_gate, w_up, w_down, block=512):
    return call(
        functools.partial(expert_kernel, block=block),
        jax.ShapeDtypeStruct(x.shape, bf16),
        x, w_gate, w_up, w_down,
        budget=36,
        scratch_shapes=[pltpu.VMEM((x.shape[0], w_gate.shape[1]), bf16)],
    )


def combine_kernel(
    tokens_ref, slots_ref, weights_ref, back_ref, lengths_ref, hidden_ref, embedded_ref, kept_ref, given_ref
):
    rows = tokens_ref.shape[0]
    experts = slots_ref.shape[1]
    capacity = back_ref.shape[0] // experts
    lanes = iota((rows, capacity), 1).astype(f32)
    terms = [
        jnp.where(lanes == slots_ref[:, e : e + 1], weights_ref[:, e : e + 1], 0.0)
        for e in range(experts)
    ]
    high, low = split(jnp.concatenate(terms, axis=1))
    back = back_ref[...]
    mixed = tokens_ref[...].astype(f32) + (dot(high, back) + dot(low, back))
    hidden_ref[...] = mixed.astype(bf16)
    count = lengths_ref.shape[1]
    spans = jnp.broadcast_to(lengths_ref[...], (count, count)).astype(f32)
    down, across = iota((count, count), 0), iota((count, count), 1)
    ends = jnp.sum(jnp.where(across <= down, spans, 0.0), axis=1, keepdims=True)
    sizes = jnp.sum(jnp.where(across == down, spans, 0.0), axis=1, keepdims=True)
    places = iota((count, rows), 1).astype(f32)
    member = jnp.where((places >= ends - sizes) & (places < ends), 1.0, 0.0).astype(bf16)
    first, rest = split(mixed)
    second, third = split(mixed - first.astype(f32))
    pooled = (dot(member, first) + dot(member, second) + dot(member, third)) / sizes
    embedded = pooled * lax.rsqrt(jnp.sum(pooled * pooled, axis=-1, keepdims=True) + pool_eps)
    embedded_ref[...] = embedded
    queries, documents = embedded[: count // 2], embedded[count // 2 :]
    first_core = lax.axis_index("dp") % 2 == 0
    kept_ref[...] = jnp.where(first_core, queries, documents).astype(bf16)
    given_ref[...] = jnp.where(first_core, documents, queries).astype(bf16)


def gradients(queries_ref, docs_ref, embedded_ref, first, query_grad_ref, doc_grad_ref):
    embedded = embedded_ref[...]
    count = embedded.shape[0] // 2
    total = queries_ref.shape[0]
    queries, documents = embedded[:count], embedded[count:]
    all_queries, all_docs = queries_ref[...], docs_ref[...]
    block = 256
    sums = jnp.zeros((1, total), f32)
    for at in range(0, total, block):
        scores = dot_nt(docs_ref[at : at + block, :], all_queries)
        sums = sums + jnp.sum(jnp.exp(logit_scale * scores), axis=0, keepdims=True)
    stacked = jnp.concatenate(split(embedded), axis=0)
    rows = fold(dot_nt(stacked, all_docs))[:count]
    cols = fold(dot_nt(stacked, all_queries))[count:]
    own = iota((count, total), 1) == first + iota((count, total), 0)
    pair = jnp.exp(logit_scale * jnp.sum(queries * documents, axis=-1, keepdims=True))
    rows = jnp.where(own, 0.0, jnp.exp(logit_scale * rows))
    cols = jnp.where(own, 0.0, jnp.exp(logit_scale * cols))
    row_sum = jnp.sum(rows, axis=-1, keepdims=True) + pair
    diagonal = pair / row_sum - 1.0
    likely = jnp.concatenate([rows / row_sum, cols / sums], axis=0)
    likely = jnp.concatenate(split(likely), axis=0)
    query_grad_ref[...] = logit_scale * (fold(dot(likely, all_docs))[:count] + diagonal * documents)
    doc_grad_ref[...] = logit_scale * (fold(dot(likely, all_queries))[count:] + diagonal * queries)


def gradient_kernel(mine_ref, other_ref, embedded_ref, query_grad_ref, doc_grad_ref):
    dp = lax.axis_index("dp")
    core = dp % 2
    chip = dp // 2 * lax.axis_size("expert") + lax.axis_index("expert")
    first = (chip * 2 + core) * (embedded_ref.shape[0] // 2)

    @pl.when(core == 0)
    def _():
        gradients(mine_ref, other_ref, embedded_ref, first, query_grad_ref, doc_grad_ref)

    @pl.when(core == 1)
    def _():
        gradients(other_ref, mine_ref, embedded_ref, first, query_grad_ref, doc_grad_ref)


def route(tokens, routes, norm_gain, router_weight):
    rows, width = tokens.shape
    experts = router_weight.shape[1]
    return call(
        route_kernel,
        [
            jax.ShapeDtypeStruct((rows // 2 * experts, width), bf16),
            jax.ShapeDtypeStruct((rows, experts), f32),
            jax.ShapeDtypeStruct((rows, experts), f32),
        ],
        tokens, routes.T, norm_gain, router_weight.T,
    )


def combine(tokens, slots, weights, back, lengths):
    count, width = lengths.shape[1], tokens.shape[1]
    half = jax.ShapeDtypeStruct((count // 2, width), bf16)
    return call(
        combine_kernel,
        [
            jax.ShapeDtypeStruct(tokens.shape, bf16),
            jax.ShapeDtypeStruct((count, width), f32),
            half,
            half,
        ],
        tokens, slots, weights, back, lengths,
    )


def info_nce(mine, other, embedded):
    out = jax.ShapeDtypeStruct((embedded.shape[0] // 2, embedded.shape[1]), f32)
    return call(gradient_kernel, [out, out], mine, other, embedded)


def body(tokens, routes, lengths, norm_gain, router_weight, gate_weight, up_weight, down_weight):
    width = tokens.shape[1]
    experts = router_weight.shape[1]
    outgoing, slots, weights = route(tokens, routes, norm_gain, router_weight)
    outgoing = outgoing.reshape(experts, -1, width)
    incoming = lax.all_to_all(outgoing, "expert", split_axis=0, concat_axis=0, tiled=True)
    results = expert_rows(
        incoming.reshape(-1, width), gate_weight[0], up_weight[0], down_weight[0]
    )
    results = results.reshape(experts, -1, width)
    returned = lax.all_to_all(results, "expert", split_axis=0, concat_axis=0, tiled=True)
    hidden_out, embedded, kept, given = combine(
        tokens, slots, weights, returned.reshape(-1, width), lengths
    )

    groups = lax.axis_size("dp")
    devices = groups * experts
    chips = devices // 2
    same_core = [[d for d in range(devices) if d // experts % 2 == core] for core in range(2)]
    swap = [(i, i ^ 1) for i in range(groups)]
    core = lax.axis_index("dp") % 2
    taken = lax.ppermute(given, "dp", swap)
    shard = jnp.concatenate(
        [jnp.where(core == 0, kept, taken), jnp.where(core == 0, taken, kept)]
    )
    copies = jnp.broadcast_to(shard[None], (chips,) + shard.shape)
    mine = lax.all_to_all(
        copies, ("dp", "expert"), split_axis=0, concat_axis=0, tiled=True, axis_index_groups=same_core
    ).reshape(-1, width)
    other = lax.ppermute(mine, "dp", swap)
    query_grad, doc_grad = info_nce(mine, other, embedded)
    return (hidden_out, query_grad, doc_grad)


def solution(mesh):
    placed = (
        P(("dp", "expert"), None),
        P(("dp", "expert"), None),
        P(("dp", "expert"), None),
        P(),
        P(),
        P("expert", None, None),
        P("expert", None, None),
        P("expert", None, None),
    )
    return jax.shard_map(
        body,
        mesh=mesh,
        in_specs=placed,
        out_specs=(P(("dp", "expert"), None), P(("dp", "expert"), None), P(("dp", "expert"), None)),
        check_vma=False,
    )
```

```python
import functools

import jax
import jax.numpy as jnp
from jax import lax
from jax.experimental import pallas as pl
from jax.experimental.pallas import tpu as pltpu
from jax.sharding import PartitionSpec as P

logit_scale = 50.0
norm_eps = 1e-06
pool_eps = 1e-06
f32 = jnp.float32
bf16 = jnp.bfloat16
mebibyte = 1024 * 1024


def dot(a, b):
    return jnp.dot(a, b, preferred_element_type=f32)


def dot_nt(a, b):
    return lax.dot_general(a, b, (((1,), (1,)), ((), ())), preferred_element_type=f32)


def iota(shape, axis):
    return lax.broadcasted_iota(jnp.int32, shape, axis)


def split(x):
    high = x.astype(bf16)
    return high, (x - high.astype(f32)).astype(bf16)


def fold(x):
    return x[: x.shape[0] // 2] + x[x.shape[0] // 2 :]


def call(kernel, outs, *operands, budget=16, outside=(), **options):
    whole = pl.BlockSpec(memory_space=pltpu.VMEM)
    left = pl.BlockSpec(memory_space=pltpu.HBM)
    operands = [
        pltpu.with_memory_space_constraint(x, pltpu.HBM) if at in outside else x
        for at, x in enumerate(operands)
    ]
    return pl.pallas_call(
        kernel,
        out_shape=outs,
        in_specs=[left if at in outside else whole for at in range(len(operands))],
        out_specs=jax.tree.map(lambda _: whole, outs),
        compiler_params=pltpu.CompilerParams(vmem_limit_bytes=budget * mebibyte),
        **options,
    )(*operands)


def route_kernel(
    tokens_hbm, routes_hbm, gain_hbm, router_hbm, out_ref, slots_ref, weights_ref,
    tokens_ref, routes_ref, gain_ref, router_ref, sems,
):
    copies = [
        pltpu.make_async_copy(tokens_hbm, tokens_ref, sems.at[0]),
        pltpu.make_async_copy(gain_hbm, gain_ref, sems.at[1]),
        pltpu.make_async_copy(routes_hbm, routes_ref, sems.at[2]),
        pltpu.make_async_copy(router_hbm, router_ref, sems.at[3]),
    ]
    for copy in copies:
        copy.start()
    for copy in copies:
        copy.wait()
    rows = tokens_ref.shape[0]
    experts = router_ref.shape[0]
    capacity = out_ref.shape[0] // experts
    widened = tokens_ref[...].astype(f32)
    inverse = lax.rsqrt(jnp.mean(widened * widened, axis=-1, keepdims=True) + norm_eps)
    normed = (widened * inverse * gain_ref[...]).astype(bf16)
    labels = iota((experts, rows), 0)
    hit = (routes_ref[0:1, :] == labels) | (routes_ref[1:2, :] == labels)
    hits = jnp.where(hit, 1.0, 0.0).astype(bf16)
    down, across = iota((rows, rows), 0), iota((rows, rows), 1)
    ranks = dot(hits, jnp.where(down < across, 1.0, 0.0).astype(bf16))
    ranks = jnp.where(hit, ranks, -1.0)
    places = iota((capacity, rows), 0).astype(f32)
    for e in range(experts):
        chosen = jnp.where(places == ranks[e : e + 1, :], 1.0, 0.0).astype(bf16)
        out_ref[e * capacity : (e + 1) * capacity, :] = dot(chosen, normed).astype(bf16)
    hits_down = dot_nt(jnp.where(down == across, 1.0, 0.0).astype(bf16), hits)
    ranks_down = dot_nt(jnp.where(across < down, 1.0, 0.0).astype(bf16), hits)
    logits = dot_nt(normed, router_ref[...])
    both = jnp.sum(hits_down * logits, axis=-1, keepdims=True)
    slots_ref[...] = jnp.where(hits_down > 0.5, ranks_down, -1.0)
    weights_ref[...] = hits_down / (1.0 + jnp.exp(both - 2.0 * logits))


def expert_kernel(
    x_ref, gate_hbm, up_hbm, down_hbm, out_ref, gate_ref, up_ref, down_ref, hidden_ref, sems, *, block, ahead
):
    steps = hidden_ref.shape[1] // block

    def part(step):
        return pl.ds(pl.multiple_of(step * block, block), block)

    def fetches(step):
        at = part(step)
        return (
            pltpu.make_async_copy(gate_hbm.at[:, at], gate_ref.at[:, at], sems.at[0, step]),
            pltpu.make_async_copy(up_hbm.at[:, at], up_ref.at[:, at], sems.at[1, step]),
        )

    def down_fetch(step):
        at = part(step)
        return pltpu.make_async_copy(down_hbm.at[at, :], down_ref.at[at, :], sems.at[2, step])

    for step in range(ahead):
        for copy in fetches(step):
            copy.start()

    def columns(step, carry):
        @pl.when(step + ahead < steps)
        def _():
            for copy in fetches(step + ahead):
                copy.start()

        down_fetch(step).start()
        for copy in fetches(step):
            copy.wait()
        at = part(step)
        x = x_ref[...]
        gate_act = dot(x, gate_ref[:, at])
        up_act = dot(x, up_ref[:, at])
        hidden_ref[:, at] = (gate_act / (1.0 + jnp.exp(-gate_act)) * up_act).astype(bf16)
        return carry

    lax.fori_loop(0, steps, columns, 0)
    lax.fori_loop(0, steps, lambda step, carry: (down_fetch(step).wait(), carry)[1], 0)
    out_ref[...] = dot(hidden_ref[...], down_ref[...]).astype(bf16)


def expert_rows(x, w_gate, w_up, w_down, block=512, ahead=1):
    hidden = w_gate.shape[1]
    return call(
        functools.partial(expert_kernel, block=block, ahead=ahead),
        jax.ShapeDtypeStruct(x.shape, bf16),
        x, w_gate, w_up, w_down,
        budget=44,
        outside=(1, 2, 3),
        scratch_shapes=[
            pltpu.VMEM(w_gate.shape, bf16),
            pltpu.VMEM(w_up.shape, bf16),
            pltpu.VMEM(w_down.shape, bf16),
            pltpu.VMEM((x.shape[0], hidden), bf16),
            pltpu.SemaphoreType.DMA((3, hidden // block)),
        ],
    )


def combine_kernel(
    tokens_ref, slots_ref, weights_ref, back_ref, lengths_ref, hidden_ref, embedded_ref, kept_ref, given_ref
):
    rows = tokens_ref.shape[0]
    experts = slots_ref.shape[1]
    capacity = back_ref.shape[0] // experts
    lanes = iota((rows, capacity), 1).astype(f32)
    terms = [
        jnp.where(lanes == slots_ref[:, e : e + 1], weights_ref[:, e : e + 1], 0.0)
        for e in range(experts)
    ]
    high, low = split(jnp.concatenate(terms, axis=1))
    back = back_ref[...]
    mixed = tokens_ref[...].astype(f32) + (dot(high, back) + dot(low, back))
    hidden_ref[...] = mixed.astype(bf16)
    count = lengths_ref.shape[1]
    spans = jnp.broadcast_to(lengths_ref[...], (count, count)).astype(f32)
    down, across = iota((count, count), 0), iota((count, count), 1)
    ends = jnp.sum(jnp.where(across <= down, spans, 0.0), axis=1, keepdims=True)
    sizes = jnp.sum(jnp.where(across == down, spans, 0.0), axis=1, keepdims=True)
    places = iota((count, rows), 1).astype(f32)
    member = jnp.where((places >= ends - sizes) & (places < ends), 1.0, 0.0).astype(bf16)
    first, rest = split(mixed)
    second, third = split(mixed - first.astype(f32))
    pooled = (dot(member, first) + dot(member, second) + dot(member, third)) / sizes
    embedded = pooled * lax.rsqrt(jnp.sum(pooled * pooled, axis=-1, keepdims=True) + pool_eps)
    embedded_ref[...] = embedded
    queries, documents = embedded[: count // 2], embedded[count // 2 :]
    first_core = lax.axis_index("dp") % 2 == 0
    kept_ref[...] = jnp.where(first_core, queries, documents).astype(bf16)
    given_ref[...] = jnp.where(first_core, documents, queries).astype(bf16)


def gradients(queries_ref, docs_ref, embedded_ref, first, query_grad_ref, doc_grad_ref):
    embedded = embedded_ref[...]
    count = embedded.shape[0] // 2
    total = queries_ref.shape[0]
    queries, documents = embedded[:count], embedded[count:]
    all_queries, all_docs = queries_ref[...], docs_ref[...]
    block = 256
    sums = jnp.zeros((1, total), f32)
    for at in range(0, total, block):
        scores = dot_nt(docs_ref[at : at + block, :], all_queries)
        sums = sums + jnp.sum(jnp.exp(logit_scale * scores), axis=0, keepdims=True)
    stacked = jnp.concatenate(split(embedded), axis=0)
    rows = fold(dot_nt(stacked, all_docs))[:count]
    cols = fold(dot_nt(stacked, all_queries))[count:]
    own = iota((count, total), 1) == first + iota((count, total), 0)
    pair = jnp.exp(logit_scale * jnp.sum(queries * documents, axis=-1, keepdims=True))
    rows = jnp.where(own, 0.0, jnp.exp(logit_scale * rows))
    cols = jnp.where(own, 0.0, jnp.exp(logit_scale * cols))
    row_sum = jnp.sum(rows, axis=-1, keepdims=True) + pair
    diagonal = pair / row_sum - 1.0
    likely = jnp.concatenate([rows / row_sum, cols / sums], axis=0)
    likely = jnp.concatenate(split(likely), axis=0)
    query_grad_ref[...] = logit_scale * (fold(dot(likely, all_docs))[:count] + diagonal * documents)
    doc_grad_ref[...] = logit_scale * (fold(dot(likely, all_queries))[count:] + diagonal * queries)


def gradient_kernel(mine_ref, other_ref, embedded_ref, query_grad_ref, doc_grad_ref):
    dp = lax.axis_index("dp")
    core = dp % 2
    chip = dp // 2 * lax.axis_size("expert") + lax.axis_index("expert")
    first = (chip * 2 + core) * (embedded_ref.shape[0] // 2)

    @pl.when(core == 0)
    def _():
        gradients(mine_ref, other_ref, embedded_ref, first, query_grad_ref, doc_grad_ref)

    @pl.when(core == 1)
    def _():
        gradients(other_ref, mine_ref, embedded_ref, first, query_grad_ref, doc_grad_ref)


def route(tokens, routes, norm_gain, router_weight):
    rows, width = tokens.shape
    experts = router_weight.shape[1]
    operands = (tokens, routes.T, norm_gain, router_weight.T)
    return call(
        route_kernel,
        [
            jax.ShapeDtypeStruct((rows // 2 * experts, width), bf16),
            jax.ShapeDtypeStruct((rows, experts), f32),
            jax.ShapeDtypeStruct((rows, experts), f32),
        ],
        *operands,
        outside=(0, 1, 2, 3),
        scratch_shapes=[pltpu.VMEM(x.shape, x.dtype) for x in operands]
        + [pltpu.SemaphoreType.DMA((len(operands),))],
    )


def combine(tokens, slots, weights, back, lengths):
    count, width = lengths.shape[1], tokens.shape[1]
    half = jax.ShapeDtypeStruct((count // 2, width), bf16)
    return call(
        combine_kernel,
        [
            jax.ShapeDtypeStruct(tokens.shape, bf16),
            jax.ShapeDtypeStruct((count, width), f32),
            half,
            half,
        ],
        tokens, slots, weights, back, lengths,
    )


def info_nce(mine, other, embedded):
    out = jax.ShapeDtypeStruct((embedded.shape[0] // 2, embedded.shape[1]), f32)
    return call(gradient_kernel, [out, out], mine, other, embedded)


def body(tokens, routes, lengths, norm_gain, router_weight, gate_weight, up_weight, down_weight):
    width = tokens.shape[1]
    experts = router_weight.shape[1]
    outgoing, slots, weights = route(tokens, routes, norm_gain, router_weight)
    outgoing = outgoing.reshape(experts, -1, width)
    incoming = lax.all_to_all(outgoing, "expert", split_axis=0, concat_axis=0, tiled=True)
    results = expert_rows(
        incoming.reshape(-1, width), gate_weight[0], up_weight[0], down_weight[0]
    )
    results = results.reshape(experts, -1, width)
    returned = lax.all_to_all(results, "expert", split_axis=0, concat_axis=0, tiled=True)
    hidden_out, embedded, kept, given = combine(
        tokens, slots, weights, returned.reshape(-1, width), lengths
    )

    groups = lax.axis_size("dp")
    devices = groups * experts
    chips = devices // 2
    same_core = [[d for d in range(devices) if d // experts % 2 == core] for core in range(2)]
    swap = [(i, i ^ 1) for i in range(groups)]
    core = lax.axis_index("dp") % 2
    taken = lax.ppermute(given, "dp", swap)
    shard = jnp.concatenate(
        [jnp.where(core == 0, kept, taken), jnp.where(core == 0, taken, kept)]
    )
    copies = jnp.broadcast_to(shard[None], (chips,) + shard.shape)
    mine = lax.all_to_all(
        copies, ("dp", "expert"), split_axis=0, concat_axis=0, tiled=True, axis_index_groups=same_core
    ).reshape(-1, width)
    other = lax.ppermute(mine, "dp", swap)
    query_grad, doc_grad = info_nce(mine, other, embedded)
    return (hidden_out, query_grad, doc_grad)


def solution(mesh):
    placed = (
        P(("dp", "expert"), None),
        P(("dp", "expert"), None),
        P(("dp", "expert"), None),
        P(),
        P(),
        P("expert", None, None),
        P("expert", None, None),
        P("expert", None, None),
    )
    return jax.shard_map(
        body,
        mesh=mesh,
        in_specs=placed,
        out_specs=(P(("dp", "expert"), None), P(("dp", "expert"), None), P(("dp", "expert"), None)),
        check_vma=False,
    )
```

```python
import functools

import jax
import jax.numpy as jnp
from jax import lax
from jax.experimental import pallas as pl
from jax.experimental.pallas import tpu as pltpu
from jax.sharding import PartitionSpec as P

logit_scale = 50.0
norm_eps = 1e-06
pool_eps = 1e-06
f32 = jnp.float32
bf16 = jnp.bfloat16
mebibyte = 1024 * 1024
plane = 4
move_groups = (
    ((0, 0), (1, 0), (3, 0), (0, 1)),
    ((2, 0), (1, 1)),
    ((3, 1), (2, 1)),
)
moves = [move for group in move_groups for move in group]


def dot(a, b):
    return jnp.dot(a, b, preferred_element_type=f32)


def dot_nt(a, b):
    return lax.dot_general(a, b, (((1,), (1,)), ((), ())), preferred_element_type=f32)


def target(expert, move):
    along, across = move
    return (expert // plane + across) % 2 * plane + (expert % plane + along) % plane


def iota(shape, axis):
    return lax.broadcasted_iota(jnp.int32, shape, axis)


def split(x):
    high = x.astype(bf16)
    return high, (x - high.astype(f32)).astype(bf16)


def fold(x):
    return x[: x.shape[0] // 2] + x[x.shape[0] // 2 :]


def call(kernel, outs, *operands, budget=16, outside=(), inside=(), **options):
    whole = pl.BlockSpec(memory_space=pltpu.VMEM)
    left = pl.BlockSpec(memory_space=pltpu.HBM)
    operands = [
        pltpu.with_memory_space_constraint(x, pltpu.HBM)
        if at in outside
        else pltpu.with_memory_space_constraint(x, pltpu.VMEM)
        if at in inside
        else x
        for at, x in enumerate(operands)
    ]
    return pl.pallas_call(
        kernel,
        out_shape=outs,
        in_specs=[left if at in outside else whole for at in range(len(operands))],
        out_specs=jax.tree.map(lambda _: whole, outs),
        compiler_params=pltpu.CompilerParams(vmem_limit_bytes=budget * mebibyte),
        **options,
    )(*operands)


def route_kernel(
    tokens_hbm, routes_hbm, gain_hbm, router_hbm, *refs
):
    *out_refs, slots_ref, weights_ref, tokens_ref, routes_ref, gain_ref, router_ref, sems = refs
    copies = [
        pltpu.make_async_copy(tokens_hbm, tokens_ref, sems.at[0]),
        pltpu.make_async_copy(gain_hbm, gain_ref, sems.at[1]),
        pltpu.make_async_copy(routes_hbm, routes_ref, sems.at[2]),
        pltpu.make_async_copy(router_hbm, router_ref, sems.at[3]),
    ]
    for copy in copies:
        copy.start()
    for copy in copies:
        copy.wait()
    rows = tokens_ref.shape[0]
    experts = router_ref.shape[0]
    capacity = out_refs[0].shape[0]
    here = lax.axis_index("expert")

    def ordered(shape):
        place, labels = iota(shape, 0), jnp.zeros(shape, jnp.int32)
        for at, move in enumerate(moves):
            labels = jnp.where(place == at, target(here, move), labels)
        return labels

    widened = tokens_ref[...].astype(f32)
    inverse = lax.rsqrt(jnp.mean(widened * widened, axis=-1, keepdims=True) + norm_eps)
    normed = (widened * inverse * gain_ref[...]).astype(bf16)
    labels = ordered((experts, rows))
    hit = (routes_ref[0:1, :] == labels) | (routes_ref[1:2, :] == labels)
    hits = jnp.where(hit, 1.0, 0.0).astype(bf16)
    down, across = iota((rows, rows), 0), iota((rows, rows), 1)
    ranks = dot(hits, jnp.where(down < across, 1.0, 0.0).astype(bf16))
    ranks = jnp.where(hit, ranks, -1.0)
    places = iota((capacity, rows), 0).astype(f32)
    for e in range(experts):
        chosen = jnp.where(places == ranks[e : e + 1, :], 1.0, 0.0).astype(bf16)
        out_refs[e][...] = dot(chosen, normed).astype(bf16)
    hits_down = dot_nt(jnp.where(down == across, 1.0, 0.0).astype(bf16), hits)
    ranks_down = dot_nt(jnp.where(across < down, 1.0, 0.0).astype(bf16), hits)
    picks = ordered((experts, experts)) == iota((experts, experts), 1)
    router = dot(jnp.where(picks, 1.0, 0.0).astype(bf16), router_ref[...]).astype(bf16)
    logits = dot_nt(normed, router)
    both = jnp.sum(hits_down * logits, axis=-1, keepdims=True)
    slots_ref[...] = jnp.where(hits_down > 0.5, ranks_down, -1.0)
    weights_ref[...] = hits_down / (1.0 + jnp.exp(both - 2.0 * logits))


def stack(x_refs, x_ref):
    rows = x_refs[0].shape[0]
    for at, ref in enumerate(x_refs):
        x_ref[at * rows : (at + 1) * rows, :] = ref[...]


def unstack(x, out_refs):
    rows = out_refs[0].shape[0]
    for at, ref in enumerate(out_refs):
        ref[...] = x[at * rows : (at + 1) * rows, :]


def hidden_block(x_ref, gate_ref, up_ref, hidden_ref, at):
    x = x_ref[...]
    gate_act = dot(x, gate_ref[:, at])
    up_act = dot(x, up_ref[:, at])
    hidden_ref[:, at] = (gate_act / (1.0 + jnp.exp(-gate_act)) * up_act).astype(bf16)


def first_expert_kernel(*refs, blocks, block, ahead):
    x_refs, out_refs = refs[:blocks], refs[blocks + 3 : 2 * blocks + 3]
    gate_hbm, up_hbm, down_hbm = refs[blocks : blocks + 3]
    gate_ref, up_ref, down_ref, x_ref, hidden_ref, sems = refs[2 * blocks + 3 :]
    steps = hidden_ref.shape[1] // block

    def part(step):
        return pl.ds(pl.multiple_of(step * block, block), block)

    def fetches(step):
        at = part(step)
        return (
            pltpu.make_async_copy(gate_hbm.at[:, at], gate_ref.at[:, at], sems.at[0, step]),
            pltpu.make_async_copy(up_hbm.at[:, at], up_ref.at[:, at], sems.at[1, step]),
        )

    down_fetch = pltpu.make_async_copy(down_hbm, down_ref, sems.at[2, 0])
    for step in range(ahead):
        for copy in fetches(step):
            copy.start()
    stack(x_refs, x_ref)

    def columns(step, carry):
        @pl.when(step + ahead < steps)
        def _():
            for copy in fetches(step + ahead):
                copy.start()

        @pl.when(step + ahead == steps)
        def _():
            down_fetch.start()

        for copy in fetches(step):
            copy.wait()
        hidden_block(x_ref, gate_ref, up_ref, hidden_ref, part(step))
        return carry

    lax.fori_loop(0, steps, columns, 0)
    down_fetch.wait()
    unstack(dot(hidden_ref[...], down_ref[...]).astype(bf16), out_refs)


def later_expert_kernel(*refs, blocks, block):
    x_refs, out_refs = refs[:blocks], refs[blocks + 3 : 2 * blocks + 3]
    gate_ref, up_ref, down_ref = refs[blocks : blocks + 3]
    x_ref, hidden_ref = refs[2 * blocks + 3 :]
    stack(x_refs, x_ref)

    def columns(step, carry):
        at = pl.ds(pl.multiple_of(step * block, block), block)
        hidden_block(x_ref, gate_ref, up_ref, hidden_ref, at)
        return carry

    lax.fori_loop(0, hidden_ref.shape[1] // block, columns, 0)
    unstack(dot(hidden_ref[...], down_ref[...]).astype(bf16), out_refs)


def expert_rows(xs, weights, first, block=512, ahead=2):
    rows, width = xs[0].shape
    hidden = weights[0].shape[1]
    blocks = len(xs)
    places = range(blocks, blocks + 3)
    results = [jax.ShapeDtypeStruct(x.shape, bf16) for x in xs]
    scratch = [pltpu.VMEM((blocks * rows, width), bf16), pltpu.VMEM((blocks * rows, hidden), bf16)]
    if first:
        out = call(
            functools.partial(first_expert_kernel, blocks=blocks, block=block, ahead=ahead),
            results + [jax.ShapeDtypeStruct(w.shape, bf16) for w in weights],
            *xs, *weights,
            budget=20,
            outside=places,
            scratch_shapes=scratch + [pltpu.SemaphoreType.DMA((3, hidden // block))],
        )
        return out[:blocks], out[blocks:]
    out = call(
        functools.partial(later_expert_kernel, blocks=blocks, block=block),
        results,
        *xs, *weights,
        budget=16,
        inside=places,
        scratch_shapes=scratch,
    )
    return out, weights


def weighted_rows(slots_ref, weights_ref, back_refs, start):
    shape = slots_ref.shape[0], back_refs[0].shape[0]
    lanes = iota(shape, 1).astype(f32)
    terms = [
        jnp.where(lanes == slots_ref[:, e : e + 1], weights_ref[:, e : e + 1], 0.0)
        for e in range(start, start + len(back_refs))
    ]
    high, low = split(jnp.concatenate(terms, axis=1))
    back = jnp.concatenate([ref[...] for ref in back_refs], axis=0)
    return dot(high, back) + dot(low, back)


def early_combine_kernel(tokens_ref, slots_ref, weights_ref, *refs):
    *back_refs, mixed_ref = refs
    mixed_ref[...] = tokens_ref[...].astype(f32) + weighted_rows(slots_ref, weights_ref, back_refs, 0)


def combine_kernel(early_ref, slots_ref, weights_ref, lengths_ref, *refs):
    *back_refs, hidden_ref, embedded_ref, kept_ref, given_ref = refs
    rows = early_ref.shape[0]
    start = slots_ref.shape[1] - len(back_refs)
    mixed = early_ref[...] + weighted_rows(slots_ref, weights_ref, back_refs, start)
    hidden_ref[...] = mixed.astype(bf16)
    count = lengths_ref.shape[1]
    spans = jnp.broadcast_to(lengths_ref[...], (count, count)).astype(f32)
    down, across = iota((count, count), 0), iota((count, count), 1)
    ends = jnp.sum(jnp.where(across <= down, spans, 0.0), axis=1, keepdims=True)
    sizes = jnp.sum(jnp.where(across == down, spans, 0.0), axis=1, keepdims=True)
    places = iota((count, rows), 1).astype(f32)
    member = jnp.where((places >= ends - sizes) & (places < ends), 1.0, 0.0).astype(bf16)
    first, rest = split(mixed)
    second, third = split(mixed - first.astype(f32))
    pooled = (dot(member, first) + dot(member, second) + dot(member, third)) / sizes
    embedded = pooled * lax.rsqrt(jnp.sum(pooled * pooled, axis=-1, keepdims=True) + pool_eps)
    embedded_ref[...] = embedded
    queries, documents = embedded[: count // 2], embedded[count // 2 :]
    first_core = lax.axis_index("dp") % 2 == 0
    kept_ref[...] = jnp.where(first_core, queries, documents).astype(bf16)
    given_ref[...] = jnp.where(first_core, documents, queries).astype(bf16)


def gradients(queries_ref, docs_ref, embedded_ref, first, query_grad_ref, doc_grad_ref):
    embedded = embedded_ref[...]
    count = embedded.shape[0] // 2
    total = queries_ref.shape[0]
    queries, documents = embedded[:count], embedded[count:]
    all_queries, all_docs = queries_ref[...], docs_ref[...]
    block = 256
    sums = jnp.zeros((1, total), f32)
    for at in range(0, total, block):
        scores = dot_nt(docs_ref[at : at + block, :], all_queries)
        sums = sums + jnp.sum(jnp.exp(logit_scale * scores), axis=0, keepdims=True)
    stacked = jnp.concatenate(split(embedded), axis=0)
    rows = fold(dot_nt(stacked, all_docs))[:count]
    cols = fold(dot_nt(stacked, all_queries))[count:]
    own = iota((count, total), 1) == first + iota((count, total), 0)
    pair = jnp.exp(logit_scale * jnp.sum(queries * documents, axis=-1, keepdims=True))
    rows = jnp.where(own, 0.0, jnp.exp(logit_scale * rows))
    cols = jnp.where(own, 0.0, jnp.exp(logit_scale * cols))
    row_sum = jnp.sum(rows, axis=-1, keepdims=True) + pair
    diagonal = pair / row_sum - 1.0
    likely = jnp.concatenate([rows / row_sum, cols / sums], axis=0)
    likely = jnp.concatenate(split(likely), axis=0)
    query_grad_ref[...] = logit_scale * (fold(dot(likely, all_docs))[:count] + diagonal * documents)
    doc_grad_ref[...] = logit_scale * (fold(dot(likely, all_queries))[count:] + diagonal * queries)


def gradient_kernel(mine_ref, other_ref, embedded_ref, query_grad_ref, doc_grad_ref):
    dp = lax.axis_index("dp")
    core = dp % 2
    chip = dp // 2 * lax.axis_size("expert") + lax.axis_index("expert")
    first = (chip * 2 + core) * (embedded_ref.shape[0] // 2)

    @pl.when(core == 0)
    def _():
        gradients(mine_ref, other_ref, embedded_ref, first, query_grad_ref, doc_grad_ref)

    @pl.when(core == 1)
    def _():
        gradients(other_ref, mine_ref, embedded_ref, first, query_grad_ref, doc_grad_ref)


def route(tokens, routes, norm_gain, router_weight):
    rows, width = tokens.shape
    experts = router_weight.shape[1]
    operands = (tokens, routes.T, norm_gain, router_weight.T)
    return call(
        route_kernel,
        [
            *[jax.ShapeDtypeStruct((rows // 2, width), bf16) for _ in range(experts)],
            jax.ShapeDtypeStruct((rows, experts), f32),
            jax.ShapeDtypeStruct((rows, experts), f32),
        ],
        *operands,
        outside=(0, 1, 2, 3),
        scratch_shapes=[pltpu.VMEM(x.shape, x.dtype) for x in operands]
        + [pltpu.SemaphoreType.DMA((len(operands),))],
    )


def combine(tokens, slots, weights, backs, lengths):
    count, width = lengths.shape[1], tokens.shape[1]
    half = jax.ShapeDtypeStruct((count // 2, width), bf16)
    early = len(backs) - len(move_groups[-1])
    mixed = call(
        early_combine_kernel,
        jax.ShapeDtypeStruct(tokens.shape, f32),
        tokens, slots, weights, *backs[:early],
    )
    return call(
        combine_kernel,
        [
            jax.ShapeDtypeStruct(tokens.shape, bf16),
            jax.ShapeDtypeStruct((count, width), f32),
            half,
            half,
        ],
        mixed, slots, weights, lengths, *backs[early:],
    )


def info_nce(mine, other, embedded):
    out = jax.ShapeDtypeStruct((embedded.shape[0] // 2, embedded.shape[1]), f32)
    return call(gradient_kernel, [out, out], mine, other, embedded)


def body(tokens, routes, lengths, norm_gain, router_weight, gate_weight, up_weight, down_weight):
    width = tokens.shape[1]
    experts = router_weight.shape[1]
    *outgoing, slots, weights = route(tokens, routes, norm_gain, router_weight)

    def pairs(move, back):
        places = [(e, target(e, move)) for e in range(experts)]
        return [(to, start) for start, to in places] if back else places

    def send(x, move, back=False):
        return x if move == (0, 0) else lax.ppermute(x, "expert", pairs(move, back))

    incoming = {move: send(x, move) for move, x in zip(moves, outgoing)}
    matrices = [gate_weight[0], up_weight[0], down_weight[0]]
    backs = []
    for at, group in enumerate(move_groups):
        results, matrices = expert_rows([incoming[move] for move in group], matrices, at == 0)
        backs += [send(x, move, back=True) for move, x in zip(group, results)]
    hidden_out, embedded, kept, given = combine(tokens, slots, weights, backs, lengths)

    groups = lax.axis_size("dp")
    devices = groups * experts
    chips = devices // 2
    same_core = [[d for d in range(devices) if d // experts % 2 == core] for core in range(2)]
    swap = [(i, i ^ 1) for i in range(groups)]
    core = lax.axis_index("dp") % 2
    taken = lax.ppermute(given, "dp", swap)
    shard = jnp.concatenate(
        [jnp.where(core == 0, kept, taken), jnp.where(core == 0, taken, kept)]
    )
    copies = jnp.broadcast_to(shard[None], (chips,) + shard.shape)
    mine = lax.all_to_all(
        copies, ("dp", "expert"), split_axis=0, concat_axis=0, tiled=True, axis_index_groups=same_core
    ).reshape(-1, width)
    other = lax.ppermute(mine, "dp", swap)
    query_grad, doc_grad = info_nce(mine, other, embedded)
    return (hidden_out, query_grad, doc_grad)


def solution(mesh):
    placed = (
        P(("dp", "expert"), None),
        P(("dp", "expert"), None),
        P(("dp", "expert"), None),
        P(),
        P(),
        P("expert", None, None),
        P("expert", None, None),
        P("expert", None, None),
    )
    return jax.shard_map(
        body,
        mesh=mesh,
        in_specs=placed,
        out_specs=(P(("dp", "expert"), None), P(("dp", "expert"), None), P(("dp", "expert"), None)),
        check_vma=False,
    )
```

```python
import functools

import jax
import jax.numpy as jnp
from jax import lax
from jax.experimental import pallas as pl
from jax.experimental.pallas import tpu as pltpu
from jax.sharding import PartitionSpec as P

logit_scale = 50.0
norm_eps = 1e-06
pool_eps = 1e-06
f32 = jnp.float32
bf16 = jnp.bfloat16
mebibyte = 1024 * 1024
plane = 4
block = 512
head = 1024
move_groups = (
    ((0, 0), (1, 0), (3, 0), (0, 1)),
    ((2, 0), (1, 1)),
    ((3, 1), (2, 1)),
)
moves = [move for group in move_groups for move in group]


def dot(a, b):
    return jnp.dot(a, b, preferred_element_type=f32)


def dot_nt(a, b):
    return lax.dot_general(a, b, (((1,), (1,)), ((), ())), preferred_element_type=f32)


def target(expert, move):
    along, across = move
    return (expert // plane + across) % 2 * plane + (expert % plane + along) % plane


def iota(shape, axis):
    return lax.broadcasted_iota(jnp.int32, shape, axis)


def split(x):
    high = x.astype(bf16)
    return high, (x - high.astype(f32)).astype(bf16)


def fold(x):
    return x[: x.shape[0] // 2] + x[x.shape[0] // 2 :]


def call(kernel, outs, *operands, budget=16, outside=(), inside=(), **options):
    whole = pl.BlockSpec(memory_space=pltpu.VMEM)
    left = pl.BlockSpec(memory_space=pltpu.HBM)
    operands = [
        pltpu.with_memory_space_constraint(x, pltpu.HBM)
        if at in outside
        else pltpu.with_memory_space_constraint(x, pltpu.VMEM)
        if at in inside
        else x
        for at, x in enumerate(operands)
    ]
    return pl.pallas_call(
        kernel,
        out_shape=outs,
        in_specs=[left if at in outside else whole for at in range(len(operands))],
        out_specs=jax.tree.map(lambda _: whole, outs),
        compiler_params=pltpu.CompilerParams(vmem_limit_bytes=budget * mebibyte),
        **options,
    )(*operands)


def route_kernel(
    tokens_hbm, routes_hbm, gain_hbm, router_hbm, gate_hbm, up_hbm, *refs, head
):
    *out_refs, slots_ref, weights_ref, gate_ref, up_ref, tokens_ref, routes_ref, gain_ref, router_ref, sems = refs
    copies = [
        pltpu.make_async_copy(tokens_hbm, tokens_ref, sems.at[0]),
        pltpu.make_async_copy(gain_hbm, gain_ref, sems.at[1]),
        pltpu.make_async_copy(routes_hbm, routes_ref, sems.at[2]),
        pltpu.make_async_copy(router_hbm, router_ref, sems.at[3]),
    ]
    for copy in copies:
        copy.start()
    heads = [
        pltpu.make_async_copy(gate_hbm.at[:, :head], gate_ref.at[:, :head], sems.at[4]),
        pltpu.make_async_copy(up_hbm.at[:, :head], up_ref.at[:, :head], sems.at[5]),
    ]
    for copy in copies:
        copy.wait()
    for copy in heads:
        copy.start()
    rows = tokens_ref.shape[0]
    experts = router_ref.shape[0]
    capacity = out_refs[0].shape[0]
    here = lax.axis_index("expert")

    def ordered(shape):
        place, labels = iota(shape, 0), jnp.zeros(shape, jnp.int32)
        for at, move in enumerate(moves):
            labels = jnp.where(place == at, target(here, move), labels)
        return labels

    widened = tokens_ref[...].astype(f32)
    inverse = lax.rsqrt(jnp.mean(widened * widened, axis=-1, keepdims=True) + norm_eps)
    normed = (widened * inverse * gain_ref[...]).astype(bf16)
    labels = ordered((experts, rows))
    hit = (routes_ref[0:1, :] == labels) | (routes_ref[1:2, :] == labels)
    hits = jnp.where(hit, 1.0, 0.0).astype(bf16)
    down, across = iota((rows, rows), 0), iota((rows, rows), 1)
    ranks = dot(hits, jnp.where(down < across, 1.0, 0.0).astype(bf16))
    ranks = jnp.where(hit, ranks, -1.0)
    places = iota((capacity, rows), 0).astype(f32)
    for e in range(experts):
        chosen = jnp.where(places == ranks[e : e + 1, :], 1.0, 0.0).astype(bf16)
        out_refs[e][...] = dot(chosen, normed).astype(bf16)
    hits_down = dot_nt(jnp.where(down == across, 1.0, 0.0).astype(bf16), hits)
    ranks_down = dot_nt(jnp.where(across < down, 1.0, 0.0).astype(bf16), hits)
    picks = ordered((experts, experts)) == iota((experts, experts), 1)
    router = dot(jnp.where(picks, 1.0, 0.0).astype(bf16), router_ref[...]).astype(bf16)
    logits = dot_nt(normed, router)
    both = jnp.sum(hits_down * logits, axis=-1, keepdims=True)
    slots_ref[...] = jnp.where(hits_down > 0.5, ranks_down, -1.0)
    weights_ref[...] = hits_down / (1.0 + jnp.exp(both - 2.0 * logits))
    for copy in heads:
        copy.wait()


def stack(x_refs, x_ref):
    rows = x_refs[0].shape[0]
    for at, ref in enumerate(x_refs):
        x_ref[at * rows : (at + 1) * rows, :] = ref[...]


def unstack(x, out_refs):
    rows = out_refs[0].shape[0]
    for at, ref in enumerate(out_refs):
        ref[...] = x[at * rows : (at + 1) * rows, :]


def hidden_block(x_ref, gate_ref, up_ref, hidden_ref, at):
    x = x_ref[...]
    gate_act = dot(x, gate_ref[:, at])
    up_act = dot(x, up_ref[:, at])
    hidden_ref[:, at] = (gate_act / (1.0 + jnp.exp(-gate_act)) * up_act).astype(bf16)


def first_expert_kernel(*refs, blocks, block, present, ahead):
    x_refs, out_refs = refs[:blocks], refs[blocks + 5 : 2 * blocks + 5]
    gate_hbm, up_hbm, down_hbm = refs[blocks : blocks + 3]
    gate_ref, up_ref, down_ref, x_ref, hidden_ref, sems = refs[2 * blocks + 5 :]
    steps = hidden_ref.shape[1] // block

    def part(step):
        return pl.ds(pl.multiple_of(step * block, block), block)

    def fetches(step):
        at = part(step)
        return (
            pltpu.make_async_copy(gate_hbm.at[:, at], gate_ref.at[:, at], sems.at[0, step]),
            pltpu.make_async_copy(up_hbm.at[:, at], up_ref.at[:, at], sems.at[1, step]),
        )

    down_fetch = pltpu.make_async_copy(down_hbm, down_ref, sems.at[2, 0])
    for step in range(present, ahead):
        for copy in fetches(step):
            copy.start()
    stack(x_refs, x_ref)

    def columns(step, carry):
        @pl.when(step + ahead < steps)
        def _():
            for copy in fetches(step + ahead):
                copy.start()

        @pl.when(step + ahead == steps)
        def _():
            down_fetch.start()

        @pl.when(step >= present)
        def _():
            for copy in fetches(step):
                copy.wait()

        hidden_block(x_ref, gate_ref, up_ref, hidden_ref, part(step))
        return carry

    lax.fori_loop(0, steps, columns, 0)
    down_fetch.wait()
    unstack(dot(hidden_ref[...], down_ref[...]).astype(bf16), out_refs)


def later_expert_kernel(*refs, blocks, block):
    x_refs, out_refs = refs[:blocks], refs[blocks + 3 : 2 * blocks + 3]
    gate_ref, up_ref, down_ref = refs[blocks : blocks + 3]
    x_ref, hidden_ref = refs[2 * blocks + 3 :]
    stack(x_refs, x_ref)

    def columns(step, carry):
        at = pl.ds(pl.multiple_of(step * block, block), block)
        hidden_block(x_ref, gate_ref, up_ref, hidden_ref, at)
        return carry

    lax.fori_loop(0, hidden_ref.shape[1] // block, columns, 0)
    unstack(dot(hidden_ref[...], down_ref[...]).astype(bf16), out_refs)


def expert_rows(xs, weights, heads, ahead=3):
    rows, width = xs[0].shape
    hidden = weights[0].shape[1]
    blocks = len(xs)
    places = range(blocks, blocks + 3)
    results = [jax.ShapeDtypeStruct(x.shape, bf16) for x in xs]
    scratch = [pltpu.VMEM((blocks * rows, width), bf16), pltpu.VMEM((blocks * rows, hidden), bf16)]
    if heads:
        out = call(
            functools.partial(
                first_expert_kernel, blocks=blocks, block=block, present=head // block, ahead=ahead
            ),
            results + [jax.ShapeDtypeStruct(w.shape, bf16) for w in weights],
            *xs, *weights, *heads,
            budget=20,
            outside=places,
            inside=range(blocks + 3, blocks + 5),
            input_output_aliases={blocks + 3: blocks, blocks + 4: blocks + 1},
            scratch_shapes=scratch + [pltpu.SemaphoreType.DMA((3, hidden // block))],
        )
        return out[:blocks], out[blocks:]
    out = call(
        functools.partial(later_expert_kernel, blocks=blocks, block=block),
        results,
        *xs, *weights,
        budget=16,
        inside=places,
        scratch_shapes=scratch,
    )
    return out, weights


def weighted_rows(slots_ref, weights_ref, back_refs, start):
    shape = slots_ref.shape[0], back_refs[0].shape[0]
    lanes = iota(shape, 1).astype(f32)
    terms = [
        jnp.where(lanes == slots_ref[:, e : e + 1], weights_ref[:, e : e + 1], 0.0)
        for e in range(start, start + len(back_refs))
    ]
    high, low = split(jnp.concatenate(terms, axis=1))
    back = jnp.concatenate([ref[...] for ref in back_refs], axis=0)
    return dot(high, back) + dot(low, back)


def early_combine_kernel(tokens_ref, slots_ref, weights_ref, *refs):
    *back_refs, mixed_ref = refs
    mixed_ref[...] = tokens_ref[...].astype(f32) + weighted_rows(slots_ref, weights_ref, back_refs, 0)


def combine_kernel(early_ref, slots_ref, weights_ref, lengths_ref, *refs):
    *back_refs, hidden_ref, embedded_ref, kept_ref, given_ref = refs
    rows = early_ref.shape[0]
    start = slots_ref.shape[1] - len(back_refs)
    mixed = early_ref[...] + weighted_rows(slots_ref, weights_ref, back_refs, start)
    hidden_ref[...] = mixed.astype(bf16)
    count = lengths_ref.shape[1]
    spans = jnp.broadcast_to(lengths_ref[...], (count, count)).astype(f32)
    down, across = iota((count, count), 0), iota((count, count), 1)
    ends = jnp.sum(jnp.where(across <= down, spans, 0.0), axis=1, keepdims=True)
    sizes = jnp.sum(jnp.where(across == down, spans, 0.0), axis=1, keepdims=True)
    places = iota((count, rows), 1).astype(f32)
    member = jnp.where((places >= ends - sizes) & (places < ends), 1.0, 0.0).astype(bf16)
    first, rest = split(mixed)
    second, third = split(mixed - first.astype(f32))
    pooled = (dot(member, first) + dot(member, second) + dot(member, third)) / sizes
    embedded = pooled * lax.rsqrt(jnp.sum(pooled * pooled, axis=-1, keepdims=True) + pool_eps)
    embedded_ref[...] = embedded
    queries, documents = embedded[: count // 2], embedded[count // 2 :]
    first_core = lax.axis_index("dp") % 2 == 0
    kept_ref[...] = jnp.where(first_core, queries, documents).astype(bf16)
    given_ref[...] = jnp.where(first_core, documents, queries).astype(bf16)


def gradients(queries_ref, docs_ref, embedded_ref, first, query_grad_ref, doc_grad_ref):
    embedded = embedded_ref[...]
    count = embedded.shape[0] // 2
    total = queries_ref.shape[0]
    queries, documents = embedded[:count], embedded[count:]
    all_queries, all_docs = queries_ref[...], docs_ref[...]
    block = 256
    sums = jnp.zeros((1, total), f32)
    for at in range(0, total, block):
        scores = dot_nt(docs_ref[at : at + block, :], all_queries)
        sums = sums + jnp.sum(jnp.exp(logit_scale * scores), axis=0, keepdims=True)
    stacked = jnp.concatenate(split(embedded), axis=0)
    rows = fold(dot_nt(stacked, all_docs))[:count]
    cols = fold(dot_nt(stacked, all_queries))[count:]
    own = iota((count, total), 1) == first + iota((count, total), 0)
    pair = jnp.exp(logit_scale * jnp.sum(queries * documents, axis=-1, keepdims=True))
    rows = jnp.where(own, 0.0, jnp.exp(logit_scale * rows))
    cols = jnp.where(own, 0.0, jnp.exp(logit_scale * cols))
    row_sum = jnp.sum(rows, axis=-1, keepdims=True) + pair
    diagonal = pair / row_sum - 1.0
    likely = jnp.concatenate([rows / row_sum, cols / sums], axis=0)
    likely = jnp.concatenate(split(likely), axis=0)
    query_grad_ref[...] = logit_scale * (fold(dot(likely, all_docs))[:count] + diagonal * documents)
    doc_grad_ref[...] = logit_scale * (fold(dot(likely, all_queries))[count:] + diagonal * queries)


def gradient_kernel(mine_ref, other_ref, embedded_ref, query_grad_ref, doc_grad_ref):
    dp = lax.axis_index("dp")
    core = dp % 2
    chip = dp // 2 * lax.axis_size("expert") + lax.axis_index("expert")
    first = (chip * 2 + core) * (embedded_ref.shape[0] // 2)

    @pl.when(core == 0)
    def _():
        gradients(mine_ref, other_ref, embedded_ref, first, query_grad_ref, doc_grad_ref)

    @pl.when(core == 1)
    def _():
        gradients(other_ref, mine_ref, embedded_ref, first, query_grad_ref, doc_grad_ref)


def route(tokens, routes, norm_gain, router_weight, gate, up):
    rows, width = tokens.shape
    experts = router_weight.shape[1]
    operands = (tokens, routes.T, norm_gain, router_weight.T, gate, up)
    return call(
        functools.partial(route_kernel, head=head),
        [
            *[jax.ShapeDtypeStruct((rows // 2, width), bf16) for _ in range(experts)],
            jax.ShapeDtypeStruct((rows, experts), f32),
            jax.ShapeDtypeStruct((rows, experts), f32),
            jax.ShapeDtypeStruct(gate.shape, bf16),
            jax.ShapeDtypeStruct(up.shape, bf16),
        ],
        *operands,
        outside=range(6),
        scratch_shapes=[pltpu.VMEM(x.shape, x.dtype) for x in operands[:4]]
        + [pltpu.SemaphoreType.DMA((len(operands),))],
    )


def combine(tokens, slots, weights, backs, lengths):
    count, width = lengths.shape[1], tokens.shape[1]
    half = jax.ShapeDtypeStruct((count // 2, width), bf16)
    early = len(backs) - len(move_groups[-1])
    mixed = call(
        early_combine_kernel,
        jax.ShapeDtypeStruct(tokens.shape, f32),
        tokens, slots, weights, *backs[:early],
    )
    return call(
        combine_kernel,
        [
            jax.ShapeDtypeStruct(tokens.shape, bf16),
            jax.ShapeDtypeStruct((count, width), f32),
            half,
            half,
        ],
        mixed, slots, weights, lengths, *backs[early:],
    )


def info_nce(mine, other, embedded):
    out = jax.ShapeDtypeStruct((embedded.shape[0] // 2, embedded.shape[1]), f32)
    return call(gradient_kernel, [out, out], mine, other, embedded)


def body(tokens, routes, lengths, norm_gain, router_weight, gate_weight, up_weight, down_weight):
    width = tokens.shape[1]
    experts = router_weight.shape[1]
    matrices = [gate_weight[0], up_weight[0], down_weight[0]]
    *outgoing, slots, weights, gate, up = route(
        tokens, routes, norm_gain, router_weight, *matrices[:2]
    )

    def pairs(move, back):
        places = [(e, target(e, move)) for e in range(experts)]
        return [(to, start) for start, to in places] if back else places

    def send(x, move, back=False):
        return x if move == (0, 0) else lax.ppermute(x, "expert", pairs(move, back))

    incoming = {move: send(x, move) for move, x in zip(moves, outgoing)}
    backs, heads = [], [gate, up]
    for group in move_groups:
        results, matrices = expert_rows([incoming[move] for move in group], matrices, heads)
        heads = []
        backs += [send(x, move, back=True) for move, x in zip(group, results)]
    hidden_out, embedded, kept, given = combine(tokens, slots, weights, backs, lengths)

    groups = lax.axis_size("dp")
    devices = groups * experts
    chips = devices // 2
    same_core = [[d for d in range(devices) if d // experts % 2 == core] for core in range(2)]
    swap = [(i, i ^ 1) for i in range(groups)]
    core = lax.axis_index("dp") % 2
    taken = lax.ppermute(given, "dp", swap)
    shard = jnp.concatenate(
        [jnp.where(core == 0, kept, taken), jnp.where(core == 0, taken, kept)]
    )
    copies = jnp.broadcast_to(shard[None], (chips,) + shard.shape)
    mine = lax.all_to_all(
        copies, ("dp", "expert"), split_axis=0, concat_axis=0, tiled=True, axis_index_groups=same_core
    ).reshape(-1, width)
    other = lax.ppermute(mine, "dp", swap)
    query_grad, doc_grad = info_nce(mine, other, embedded)
    return (hidden_out, query_grad, doc_grad)


def solution(mesh):
    placed = (
        P(("dp", "expert"), None),
        P(("dp", "expert"), None),
        P(("dp", "expert"), None),
        P(),
        P(),
        P("expert", None, None),
        P("expert", None, None),
        P("expert", None, None),
    )
    return jax.shard_map(
        body,
        mesh=mesh,
        in_specs=placed,
        out_specs=(P(("dp", "expert"), None), P(("dp", "expert"), None), P(("dp", "expert"), None)),
        check_vma=False,
    )
```

```python
import functools

import jax
import jax.numpy as jnp
from jax import lax
from jax.experimental import pallas as pl
from jax.experimental.pallas import tpu as pltpu
from jax.sharding import PartitionSpec as P

logit_scale = 50.0
norm_eps = 1e-06
pool_eps = 1e-06
f32 = jnp.float32
bf16 = jnp.bfloat16
mebibyte = 1024 * 1024
plane = 4
line = 4
move_groups = (
    ((0, 0), (1, 0), (3, 0), (0, 1)),
    ((2, 0), (1, 1)),
    ((3, 1), (2, 1)),
)
moves = [move for group in move_groups for move in group]


def dot(a, b):
    return jnp.dot(a, b, preferred_element_type=f32)


def dot_nt(a, b):
    return lax.dot_general(a, b, (((1,), (1,)), ((), ())), preferred_element_type=f32)


def target(expert, move):
    along, across = move
    return (expert // plane + across) % 2 * plane + (expert % plane + along) % plane


def iota(shape, axis):
    return lax.broadcasted_iota(jnp.int32, shape, axis)


def split(x):
    high = x.astype(bf16)
    return high, (x - high.astype(f32)).astype(bf16)


def fold(x):
    return x[: x.shape[0] // 2] + x[x.shape[0] // 2 :]


def call(kernel, outs, *operands, budget=16, outside=(), inside=(), **options):
    whole = pl.BlockSpec(memory_space=pltpu.VMEM)
    left = pl.BlockSpec(memory_space=pltpu.HBM)
    operands = [
        pltpu.with_memory_space_constraint(x, pltpu.HBM)
        if at in outside
        else pltpu.with_memory_space_constraint(x, pltpu.VMEM)
        if at in inside
        else x
        for at, x in enumerate(operands)
    ]
    return pl.pallas_call(
        kernel,
        out_shape=outs,
        in_specs=[left if at in outside else whole for at in range(len(operands))],
        out_specs=jax.tree.map(lambda _: whole, outs),
        compiler_params=pltpu.CompilerParams(vmem_limit_bytes=budget * mebibyte),
        **options,
    )(*operands)


def route_kernel(
    tokens_hbm, routes_hbm, gain_hbm, router_hbm, *refs
):
    *out_refs, slots_ref, weights_ref, tokens_ref, routes_ref, gain_ref, router_ref, sems = refs
    copies = [
        pltpu.make_async_copy(tokens_hbm, tokens_ref, sems.at[0]),
        pltpu.make_async_copy(gain_hbm, gain_ref, sems.at[1]),
        pltpu.make_async_copy(routes_hbm, routes_ref, sems.at[2]),
        pltpu.make_async_copy(router_hbm, router_ref, sems.at[3]),
    ]
    for copy in copies:
        copy.start()
    for copy in copies:
        copy.wait()
    rows = tokens_ref.shape[0]
    experts = router_ref.shape[0]
    capacity = out_refs[0].shape[0]
    here = lax.axis_index("expert")

    def ordered(shape):
        place, labels = iota(shape, 0), jnp.zeros(shape, jnp.int32)
        for at, move in enumerate(moves):
            labels = jnp.where(place == at, target(here, move), labels)
        return labels

    widened = tokens_ref[...].astype(f32)
    inverse = lax.rsqrt(jnp.mean(widened * widened, axis=-1, keepdims=True) + norm_eps)
    normed = (widened * inverse * gain_ref[...]).astype(bf16)
    labels = ordered((experts, rows))
    hit = (routes_ref[0:1, :] == labels) | (routes_ref[1:2, :] == labels)
    hits = jnp.where(hit, 1.0, 0.0).astype(bf16)
    down, across = iota((rows, rows), 0), iota((rows, rows), 1)
    ranks = dot(hits, jnp.where(down < across, 1.0, 0.0).astype(bf16))
    ranks = jnp.where(hit, ranks, -1.0)
    places = iota((capacity, rows), 0).astype(f32)
    for e in range(experts):
        chosen = jnp.where(places == ranks[e : e + 1, :], 1.0, 0.0).astype(bf16)
        out_refs[e][...] = dot(chosen, normed).astype(bf16)
    hits_down = dot_nt(jnp.where(down == across, 1.0, 0.0).astype(bf16), hits)
    ranks_down = dot_nt(jnp.where(across < down, 1.0, 0.0).astype(bf16), hits)
    picks = ordered((experts, experts)) == iota((experts, experts), 1)
    router = dot(jnp.where(picks, 1.0, 0.0).astype(bf16), router_ref[...]).astype(bf16)
    logits = dot_nt(normed, router)
    both = jnp.sum(hits_down * logits, axis=-1, keepdims=True)
    slots_ref[...] = jnp.where(hits_down > 0.5, ranks_down, -1.0)
    weights_ref[...] = hits_down / (1.0 + jnp.exp(both - 2.0 * logits))


def stack(x_refs, x_ref):
    rows = x_refs[0].shape[0]
    for at, ref in enumerate(x_refs):
        x_ref[at * rows : (at + 1) * rows, :] = ref[...]


def unstack(x, out_refs):
    rows = out_refs[0].shape[0]
    for at, ref in enumerate(out_refs):
        ref[...] = x[at * rows : (at + 1) * rows, :]


def hidden_block(x_ref, gate_ref, up_ref, hidden_ref, at):
    x = x_ref[...]
    gate_act = dot(x, gate_ref[:, at])
    up_act = dot(x, up_ref[:, at])
    hidden_ref[:, at] = (gate_act / (1.0 + jnp.exp(-gate_act)) * up_act).astype(bf16)


def first_expert_kernel(*refs, blocks, block, ahead):
    x_refs, out_refs = refs[:blocks], refs[blocks + 3 : 2 * blocks + 3]
    gate_hbm, up_hbm, down_hbm = refs[blocks : blocks + 3]
    gate_ref, up_ref, down_ref, x_ref, hidden_ref, sems = refs[2 * blocks + 3 :]
    steps = hidden_ref.shape[1] // block

    def part(step):
        return pl.ds(pl.multiple_of(step * block, block), block)

    def fetches(step):
        at = part(step)
        return (
            pltpu.make_async_copy(gate_hbm.at[:, at], gate_ref.at[:, at], sems.at[0, step]),
            pltpu.make_async_copy(up_hbm.at[:, at], up_ref.at[:, at], sems.at[1, step]),
        )

    down_fetch = pltpu.make_async_copy(down_hbm, down_ref, sems.at[2, 0])
    for step in range(ahead):
        for copy in fetches(step):
            copy.start()
    stack(x_refs, x_ref)

    def columns(step, carry):
        @pl.when(step + ahead < steps)
        def _():
            for copy in fetches(step + ahead):
                copy.start()

        @pl.when(step + ahead == steps)
        def _():
            down_fetch.start()

        for copy in fetches(step):
            copy.wait()
        hidden_block(x_ref, gate_ref, up_ref, hidden_ref, part(step))
        return carry

    lax.fori_loop(0, steps, columns, 0)
    down_fetch.wait()
    unstack(dot(hidden_ref[...], down_ref[...]).astype(bf16), out_refs)


def later_expert_kernel(*refs, blocks, block):
    x_refs, out_refs = refs[:blocks], refs[blocks + 3 : 2 * blocks + 3]
    gate_ref, up_ref, down_ref = refs[blocks : blocks + 3]
    x_ref, hidden_ref = refs[2 * blocks + 3 :]
    stack(x_refs, x_ref)

    def columns(step, carry):
        at = pl.ds(pl.multiple_of(step * block, block), block)
        hidden_block(x_ref, gate_ref, up_ref, hidden_ref, at)
        return carry

    lax.fori_loop(0, hidden_ref.shape[1] // block, columns, 0)
    unstack(dot(hidden_ref[...], down_ref[...]).astype(bf16), out_refs)


def expert_rows(xs, weights, first, block=512, ahead=2):
    rows, width = xs[0].shape
    hidden = weights[0].shape[1]
    blocks = len(xs)
    places = range(blocks, blocks + 3)
    results = [jax.ShapeDtypeStruct(x.shape, bf16) for x in xs]
    scratch = [pltpu.VMEM((blocks * rows, width), bf16), pltpu.VMEM((blocks * rows, hidden), bf16)]
    if first:
        out = call(
            functools.partial(first_expert_kernel, blocks=blocks, block=block, ahead=ahead),
            results + [jax.ShapeDtypeStruct(w.shape, bf16) for w in weights],
            *xs, *weights,
            budget=20,
            outside=places,
            scratch_shapes=scratch + [pltpu.SemaphoreType.DMA((3, hidden // block))],
        )
        return out[:blocks], out[blocks:]
    out = call(
        functools.partial(later_expert_kernel, blocks=blocks, block=block),
        results,
        *xs, *weights,
        budget=16,
        inside=places,
        scratch_shapes=scratch,
    )
    return out, weights


def weighted_rows(slots_ref, weights_ref, back_refs, start):
    shape = slots_ref.shape[0], back_refs[0].shape[0]
    lanes = iota(shape, 1).astype(f32)
    terms = [
        jnp.where(lanes == slots_ref[:, e : e + 1], weights_ref[:, e : e + 1], 0.0)
        for e in range(start, start + len(back_refs))
    ]
    high, low = split(jnp.concatenate(terms, axis=1))
    back = jnp.concatenate([ref[...] for ref in back_refs], axis=0)
    return dot(high, back) + dot(low, back)


def early_combine_kernel(tokens_ref, slots_ref, weights_ref, *refs):
    *back_refs, mixed_ref = refs
    mixed_ref[...] = tokens_ref[...].astype(f32) + weighted_rows(slots_ref, weights_ref, back_refs, 0)


def combine_kernel(early_ref, slots_ref, weights_ref, lengths_ref, *refs):
    *back_refs, hidden_ref, embedded_ref, kept_ref, given_ref = refs
    rows = early_ref.shape[0]
    start = slots_ref.shape[1] - len(back_refs)
    mixed = early_ref[...] + weighted_rows(slots_ref, weights_ref, back_refs, start)
    hidden_ref[...] = mixed.astype(bf16)
    count = lengths_ref.shape[1]
    spans = jnp.broadcast_to(lengths_ref[...], (count, count)).astype(f32)
    down, across = iota((count, count), 0), iota((count, count), 1)
    ends = jnp.sum(jnp.where(across <= down, spans, 0.0), axis=1, keepdims=True)
    sizes = jnp.sum(jnp.where(across == down, spans, 0.0), axis=1, keepdims=True)
    places = iota((count, rows), 1).astype(f32)
    member = jnp.where((places >= ends - sizes) & (places < ends), 1.0, 0.0).astype(bf16)
    first, rest = split(mixed)
    second, third = split(mixed - first.astype(f32))
    pooled = (dot(member, first) + dot(member, second) + dot(member, third)) / sizes
    embedded = pooled * lax.rsqrt(jnp.sum(pooled * pooled, axis=-1, keepdims=True) + pool_eps)
    embedded_ref[...] = embedded
    queries, documents = embedded[: count // 2], embedded[count // 2 :]
    first_core = lax.axis_index("dp") % 2 == 0
    kept_ref[...] = jnp.where(first_core, queries, documents).astype(bf16)
    given_ref[...] = jnp.where(first_core, documents, queries).astype(bf16)


def gradients(queries_ref, docs_ref, embedded_ref, first, query_grad_ref, doc_grad_ref):
    embedded = embedded_ref[...]
    count = embedded.shape[0] // 2
    total = queries_ref.shape[0]
    queries, documents = embedded[:count], embedded[count:]
    all_queries, all_docs = queries_ref[...], docs_ref[...]
    block = 256
    sums = jnp.zeros((1, total), f32)
    for at in range(0, total, block):
        scores = dot_nt(docs_ref[at : at + block, :], all_queries)
        sums = sums + jnp.sum(jnp.exp(logit_scale * scores), axis=0, keepdims=True)
    stacked = jnp.concatenate(split(embedded), axis=0)
    rows = fold(dot_nt(stacked, all_docs))[:count]
    cols = fold(dot_nt(stacked, all_queries))[count:]
    own = iota((count, total), 1) == first + iota((count, total), 0)
    pair = jnp.exp(logit_scale * jnp.sum(queries * documents, axis=-1, keepdims=True))
    rows = jnp.where(own, 0.0, jnp.exp(logit_scale * rows))
    cols = jnp.where(own, 0.0, jnp.exp(logit_scale * cols))
    row_sum = jnp.sum(rows, axis=-1, keepdims=True) + pair
    diagonal = pair / row_sum - 1.0
    likely = jnp.concatenate([rows / row_sum, cols / sums], axis=0)
    likely = jnp.concatenate(split(likely), axis=0)
    query_grad_ref[...] = logit_scale * (fold(dot(likely, all_docs))[:count] + diagonal * documents)
    doc_grad_ref[...] = logit_scale * (fold(dot(likely, all_queries))[count:] + diagonal * queries)


def gradient_kernel(mine_ref, other_ref, embedded_ref, query_grad_ref, doc_grad_ref):
    dp = lax.axis_index("dp")
    core = dp % 2
    rank = dp // 2 * (lax.axis_size("expert") // plane) + lax.axis_index("expert") // plane
    first = (rank * 2 + core) * (embedded_ref.shape[0] // 2)

    @pl.when(core == 0)
    def _():
        gradients(mine_ref, other_ref, embedded_ref, first, query_grad_ref, doc_grad_ref)

    @pl.when(core == 1)
    def _():
        gradients(other_ref, mine_ref, embedded_ref, first, query_grad_ref, doc_grad_ref)


def route(tokens, routes, norm_gain, router_weight):
    rows, width = tokens.shape
    experts = router_weight.shape[1]
    operands = (tokens, routes.T, norm_gain, router_weight.T)
    return call(
        route_kernel,
        [
            *[jax.ShapeDtypeStruct((rows // 2, width), bf16) for _ in range(experts)],
            jax.ShapeDtypeStruct((rows, experts), f32),
            jax.ShapeDtypeStruct((rows, experts), f32),
        ],
        *operands,
        outside=(0, 1, 2, 3),
        scratch_shapes=[pltpu.VMEM(x.shape, x.dtype) for x in operands]
        + [pltpu.SemaphoreType.DMA((len(operands),))],
    )


def combine(tokens, slots, weights, backs, lengths):
    count, width = lengths.shape[1], tokens.shape[1]
    half = jax.ShapeDtypeStruct((count // 2, width), bf16)
    early = len(backs) - len(move_groups[-1])
    mixed = call(
        early_combine_kernel,
        jax.ShapeDtypeStruct(tokens.shape, f32),
        tokens, slots, weights, *backs[:early],
    )
    return call(
        combine_kernel,
        [
            jax.ShapeDtypeStruct(tokens.shape, bf16),
            jax.ShapeDtypeStruct((count, width), f32),
            half,
            half,
        ],
        mixed, slots, weights, lengths, *backs[early:],
    )


def info_nce(mine, other, embedded):
    out = jax.ShapeDtypeStruct((embedded.shape[0] // 2, embedded.shape[1]), f32)
    return call(gradient_kernel, [out, out], mine, other, embedded)


def body(tokens, routes, lengths, norm_gain, router_weight, gate_weight, up_weight, down_weight):
    width = tokens.shape[1]
    experts = router_weight.shape[1]
    *outgoing, slots, weights = route(tokens, routes, norm_gain, router_weight)

    def pairs(move, back):
        places = [(e, target(e, move)) for e in range(experts)]
        return [(to, start) for start, to in places] if back else places

    def send(x, move, back=False):
        return x if move == (0, 0) else lax.ppermute(x, "expert", pairs(move, back))

    incoming = {move: send(x, move) for move, x in zip(moves, outgoing)}
    matrices = [gate_weight[0], up_weight[0], down_weight[0]]
    backs = []
    for at, group in enumerate(move_groups):
        results, matrices = expert_rows([incoming[move] for move in group], matrices, at == 0)
        backs += [send(x, move, back=True) for move, x in zip(group, results)]
    hidden_out, embedded, kept, given = combine(tokens, slots, weights, backs, lengths)

    groups = lax.axis_size("dp")
    swap = [(i, i ^ 1) for i in range(groups)]
    core = lax.axis_index("dp") % 2
    taken = lax.ppermute(given, "dp", swap)
    shard = jnp.concatenate(
        [jnp.where(core == 0, kept, taken), jnp.where(core == 0, taken, kept)]
    )
    colours = [[] for _ in range(2 * plane)]
    for device in range(groups * experts):
        dp, expert = divmod(device, experts)
        colours[(expert + 2 * (dp // line)) % plane * 2 + dp % 2].append(device)
    copies = jnp.broadcast_to(shard[None], (len(colours[0]),) + shard.shape)
    own = lax.all_to_all(
        copies, ("dp", "expert"), split_axis=0, concat_axis=0, tiled=True, axis_index_groups=colours
    ).reshape(-1, width)
    blocks = [
        own,
        lax.ppermute(own, "expert", pairs((3, 0), False)),
        lax.ppermute(own, "dp", [(i, (i - line) % groups) for i in range(groups)]),
        lax.ppermute(own, "expert", pairs((1, 0), False)),
    ]
    mine = jnp.concatenate(blocks)
    other = jnp.concatenate([lax.ppermute(x, "dp", swap) for x in blocks])
    query_grad, doc_grad = info_nce(mine, other, embedded)
    return (hidden_out, query_grad, doc_grad)


def solution(mesh):
    placed = (
        P(("dp", "expert"), None),
        P(("dp", "expert"), None),
        P(("dp", "expert"), None),
        P(),
        P(),
        P("expert", None, None),
        P("expert", None, None),
        P("expert", None, None),
    )
    return jax.shard_map(
        body,
        mesh=mesh,
        in_specs=placed,
        out_specs=(P(("dp", "expert"), None), P(("dp", "expert"), None), P(("dp", "expert"), None)),
        check_vma=False,
    )
```

```python
import functools

import jax
import jax.numpy as jnp
from jax import lax
from jax.experimental import pallas as pl
from jax.experimental.pallas import tpu as pltpu
from jax.sharding import PartitionSpec as P

logit_scale = 50.0
norm_eps = 1e-06
pool_eps = 1e-06
f32 = jnp.float32
bf16 = jnp.bfloat16
mebibyte = 1024 * 1024
plane = 4
line = 4
move_groups = (
    ((0, 0), (1, 0), (3, 0), (0, 1)),
    ((2, 0), (1, 1)),
    ((3, 1), (2, 1)),
)
moves = [move for group in move_groups for move in group]


def dot(a, b):
    return jnp.dot(a, b, preferred_element_type=f32)


def dot_nt(a, b):
    return lax.dot_general(a, b, (((1,), (1,)), ((), ())), preferred_element_type=f32)


def target(expert, move):
    along, across = move
    return (expert // plane + across) % 2 * plane + (expert % plane + along) % plane


def iota(shape, axis):
    return lax.broadcasted_iota(jnp.int32, shape, axis)


def split(x):
    high = x.astype(bf16)
    return high, (x - high.astype(f32)).astype(bf16)


def fold(x):
    return x[: x.shape[0] // 2] + x[x.shape[0] // 2 :]


def call(kernel, outs, *operands, budget=16, outside=(), inside=(), **options):
    whole = pl.BlockSpec(memory_space=pltpu.VMEM)
    left = pl.BlockSpec(memory_space=pltpu.HBM)
    operands = [
        pltpu.with_memory_space_constraint(x, pltpu.HBM)
        if at in outside
        else pltpu.with_memory_space_constraint(x, pltpu.VMEM)
        if at in inside
        else x
        for at, x in enumerate(operands)
    ]
    return pl.pallas_call(
        kernel,
        out_shape=outs,
        in_specs=[left if at in outside else whole for at in range(len(operands))],
        out_specs=jax.tree.map(lambda _: whole, outs),
        compiler_params=pltpu.CompilerParams(vmem_limit_bytes=budget * mebibyte),
        **options,
    )(*operands)


def route_kernel(
    tokens_hbm, routes_hbm, gain_hbm, router_hbm, *refs
):
    *out_refs, slots_ref, weights_ref, tokens_ref, routes_ref, gain_ref, router_ref, sems = refs
    copies = [
        pltpu.make_async_copy(tokens_hbm, tokens_ref, sems.at[0]),
        pltpu.make_async_copy(gain_hbm, gain_ref, sems.at[1]),
        pltpu.make_async_copy(routes_hbm, routes_ref, sems.at[2]),
        pltpu.make_async_copy(router_hbm, router_ref, sems.at[3]),
    ]
    for copy in copies:
        copy.start()
    for copy in copies:
        copy.wait()
    rows = tokens_ref.shape[0]
    experts = router_ref.shape[0]
    capacity = out_refs[0].shape[0]
    here = lax.axis_index("expert")

    def ordered(shape):
        place, labels = iota(shape, 0), jnp.zeros(shape, jnp.int32)
        for at, move in enumerate(moves):
            labels = jnp.where(place == at, target(here, move), labels)
        return labels

    widened = tokens_ref[...].astype(f32)
    inverse = lax.rsqrt(jnp.mean(widened * widened, axis=-1, keepdims=True) + norm_eps)
    normed = (widened * inverse * gain_ref[...]).astype(bf16)
    labels = ordered((experts, rows))
    hit = (routes_ref[0:1, :] == labels) | (routes_ref[1:2, :] == labels)
    hits = jnp.where(hit, 1.0, 0.0).astype(bf16)
    down, across = iota((rows, rows), 0), iota((rows, rows), 1)
    ranks = dot(hits, jnp.where(down < across, 1.0, 0.0).astype(bf16))
    ranks = jnp.where(hit, ranks, -1.0)
    places = iota((capacity, rows), 0).astype(f32)
    for e in range(experts):
        chosen = jnp.where(places == ranks[e : e + 1, :], 1.0, 0.0).astype(bf16)
        out_refs[e][...] = dot(chosen, normed).astype(bf16)
    hits_down = dot_nt(jnp.where(down == across, 1.0, 0.0).astype(bf16), hits)
    ranks_down = dot_nt(jnp.where(across < down, 1.0, 0.0).astype(bf16), hits)
    picks = ordered((experts, experts)) == iota((experts, experts), 1)
    router = dot(jnp.where(picks, 1.0, 0.0).astype(bf16), router_ref[...]).astype(bf16)
    logits = dot_nt(normed, router)
    both = jnp.sum(hits_down * logits, axis=-1, keepdims=True)
    slots_ref[...] = jnp.where(hits_down > 0.5, ranks_down, -1.0)
    weights_ref[...] = hits_down / (1.0 + jnp.exp(both - 2.0 * logits))


def stack(x_refs, x_ref):
    rows = x_refs[0].shape[0]
    for at, ref in enumerate(x_refs):
        x_ref[at * rows : (at + 1) * rows, :] = ref[...]


def unstack(x, out_refs):
    rows = out_refs[0].shape[0]
    for at, ref in enumerate(out_refs):
        ref[...] = x[at * rows : (at + 1) * rows, :]


def hidden_block(x_ref, gate_ref, up_ref, hidden_ref, at):
    x = x_ref[...]
    gate_act = dot(x, gate_ref[:, at])
    up_act = dot(x, up_ref[:, at])
    hidden_ref[:, at] = (gate_act / (1.0 + jnp.exp(-gate_act)) * up_act).astype(bf16)


def first_expert_kernel(*refs, blocks, block, ahead):
    x_refs, out_refs = refs[:blocks], refs[blocks + 3 : 2 * blocks + 3]
    gate_hbm, up_hbm, down_hbm = refs[blocks : blocks + 3]
    gate_ref, up_ref, down_ref, x_ref, hidden_ref, sems = refs[2 * blocks + 3 :]
    steps = hidden_ref.shape[1] // block

    def part(step):
        return pl.ds(pl.multiple_of(step * block, block), block)

    def fetches(step):
        at = part(step)
        return (
            pltpu.make_async_copy(gate_hbm.at[:, at], gate_ref.at[:, at], sems.at[0, step]),
            pltpu.make_async_copy(up_hbm.at[:, at], up_ref.at[:, at], sems.at[1, step]),
        )

    down_fetch = pltpu.make_async_copy(down_hbm, down_ref, sems.at[2, 0])
    for step in range(ahead):
        for copy in fetches(step):
            copy.start()
    stack(x_refs, x_ref)

    def columns(step, carry):
        @pl.when(step + ahead < steps)
        def _():
            for copy in fetches(step + ahead):
                copy.start()

        @pl.when(step + ahead == steps)
        def _():
            down_fetch.start()

        for copy in fetches(step):
            copy.wait()
        hidden_block(x_ref, gate_ref, up_ref, hidden_ref, part(step))
        return carry

    lax.fori_loop(0, steps, columns, 0)
    down_fetch.wait()
    unstack(dot(hidden_ref[...], down_ref[...]).astype(bf16), out_refs)


def later_expert_kernel(*refs, blocks, block):
    x_refs, out_refs = refs[:blocks], refs[blocks + 3 : 2 * blocks + 3]
    gate_ref, up_ref, down_ref = refs[blocks : blocks + 3]
    x_ref, hidden_ref = refs[2 * blocks + 3 :]
    stack(x_refs, x_ref)

    def columns(step, carry):
        at = pl.ds(pl.multiple_of(step * block, block), block)
        hidden_block(x_ref, gate_ref, up_ref, hidden_ref, at)
        return carry

    lax.fori_loop(0, hidden_ref.shape[1] // block, columns, 0)
    unstack(dot(hidden_ref[...], down_ref[...]).astype(bf16), out_refs)


def expert_rows(xs, weights, first, block=512, ahead=2):
    rows, width = xs[0].shape
    hidden = weights[0].shape[1]
    blocks = len(xs)
    places = range(blocks, blocks + 3)
    results = [jax.ShapeDtypeStruct(x.shape, bf16) for x in xs]
    scratch = [pltpu.VMEM((blocks * rows, width), bf16), pltpu.VMEM((blocks * rows, hidden), bf16)]
    if first:
        out = call(
            functools.partial(first_expert_kernel, blocks=blocks, block=block, ahead=ahead),
            results + [jax.ShapeDtypeStruct(w.shape, bf16) for w in weights],
            *xs, *weights,
            budget=20,
            outside=places,
            scratch_shapes=scratch + [pltpu.SemaphoreType.DMA((3, hidden // block))],
        )
        return out[:blocks], out[blocks:]
    out = call(
        functools.partial(later_expert_kernel, blocks=blocks, block=block),
        results,
        *xs, *weights,
        budget=16,
        inside=places,
        scratch_shapes=scratch,
    )
    return out, weights


def weighted_rows(slots_ref, weights_ref, back_refs, start):
    shape = slots_ref.shape[0], back_refs[0].shape[0]
    lanes = iota(shape, 1).astype(f32)
    terms = [
        jnp.where(lanes == slots_ref[:, e : e + 1], weights_ref[:, e : e + 1], 0.0)
        for e in range(start, start + len(back_refs))
    ]
    high, low = split(jnp.concatenate(terms, axis=1))
    back = jnp.concatenate([ref[...] for ref in back_refs], axis=0)
    return dot(high, back) + dot(low, back)


def early_combine_kernel(tokens_ref, slots_ref, weights_ref, *refs):
    *back_refs, mixed_ref = refs
    mixed_ref[...] = tokens_ref[...].astype(f32) + weighted_rows(slots_ref, weights_ref, back_refs, 0)


def combine_kernel(early_ref, slots_ref, weights_ref, lengths_ref, *refs):
    *back_refs, hidden_ref, embedded_ref, rounded_ref = refs
    rows = early_ref.shape[0]
    start = slots_ref.shape[1] - len(back_refs)
    mixed = early_ref[...] + weighted_rows(slots_ref, weights_ref, back_refs, start)
    hidden_ref[...] = mixed.astype(bf16)
    count = lengths_ref.shape[1]
    spans = jnp.broadcast_to(lengths_ref[...], (count, count)).astype(f32)
    down, across = iota((count, count), 0), iota((count, count), 1)
    ends = jnp.sum(jnp.where(across <= down, spans, 0.0), axis=1, keepdims=True)
    sizes = jnp.sum(jnp.where(across == down, spans, 0.0), axis=1, keepdims=True)
    places = iota((count, rows), 1).astype(f32)
    member = jnp.where((places >= ends - sizes) & (places < ends), 1.0, 0.0).astype(bf16)
    first, rest = split(mixed)
    second, third = split(mixed - first.astype(f32))
    pooled = (dot(member, first) + dot(member, second) + dot(member, third)) / sizes
    embedded = pooled * lax.rsqrt(jnp.sum(pooled * pooled, axis=-1, keepdims=True) + pool_eps)
    embedded_ref[...] = embedded
    rounded_ref[...] = embedded.astype(bf16)


def gradient_kernel(queries_ref, docs_ref, embedded_ref, query_grad_ref, doc_grad_ref):
    rank = lax.axis_index("dp") // 2 * (lax.axis_size("expert") // plane) + lax.axis_index("expert") // plane
    first = rank * (embedded_ref.shape[0] // 2)
    embedded = embedded_ref[...]
    count = embedded.shape[0] // 2
    total = queries_ref.shape[0]
    queries, documents = embedded[:count], embedded[count:]
    all_queries, all_docs = queries_ref[...], docs_ref[...]
    block = 256
    sums = jnp.zeros((1, total), f32)
    for at in range(0, total, block):
        scores = dot_nt(docs_ref[at : at + block, :], all_queries)
        sums = sums + jnp.sum(jnp.exp(logit_scale * scores), axis=0, keepdims=True)
    stacked = jnp.concatenate(split(embedded), axis=0)
    rows = fold(dot_nt(stacked, all_docs))[:count]
    cols = fold(dot_nt(stacked, all_queries))[count:]
    own = iota((count, total), 1) == first + iota((count, total), 0)
    pair = jnp.exp(logit_scale * jnp.sum(queries * documents, axis=-1, keepdims=True))
    rows = jnp.where(own, 0.0, jnp.exp(logit_scale * rows))
    cols = jnp.where(own, 0.0, jnp.exp(logit_scale * cols))
    row_sum = jnp.sum(rows, axis=-1, keepdims=True) + pair
    diagonal = pair / row_sum - 1.0
    likely = jnp.concatenate([rows / row_sum, cols / sums], axis=0)
    likely = jnp.concatenate(split(likely), axis=0)
    query_grad_ref[...] = logit_scale * (fold(dot(likely, all_docs))[:count] + diagonal * documents)
    doc_grad_ref[...] = logit_scale * (fold(dot(likely, all_queries))[count:] + diagonal * queries)


def route(tokens, routes, norm_gain, router_weight):
    rows, width = tokens.shape
    experts = router_weight.shape[1]
    operands = (tokens, routes.T, norm_gain, router_weight.T)
    return call(
        route_kernel,
        [
            *[jax.ShapeDtypeStruct((rows // 2, width), bf16) for _ in range(experts)],
            jax.ShapeDtypeStruct((rows, experts), f32),
            jax.ShapeDtypeStruct((rows, experts), f32),
        ],
        *operands,
        outside=(0, 1, 2, 3),
        scratch_shapes=[pltpu.VMEM(x.shape, x.dtype) for x in operands]
        + [pltpu.SemaphoreType.DMA((len(operands),))],
    )


def combine(tokens, slots, weights, backs, lengths):
    count, width = lengths.shape[1], tokens.shape[1]
    early = len(backs) - len(move_groups[-1])
    mixed = call(
        early_combine_kernel,
        jax.ShapeDtypeStruct(tokens.shape, f32),
        tokens, slots, weights, *backs[:early],
    )
    return call(
        combine_kernel,
        [
            jax.ShapeDtypeStruct(tokens.shape, bf16),
            jax.ShapeDtypeStruct((count, width), f32),
            jax.ShapeDtypeStruct((count, width), bf16),
        ],
        mixed, slots, weights, lengths, *backs[early:],
    )


def info_nce(queries, docs, embedded):
    out = jax.ShapeDtypeStruct((embedded.shape[0] // 2, embedded.shape[1]), f32)
    return call(gradient_kernel, [out, out], queries, docs, embedded)


def body(tokens, routes, lengths, norm_gain, router_weight, gate_weight, up_weight, down_weight):
    width = tokens.shape[1]
    experts = router_weight.shape[1]
    *outgoing, slots, weights = route(tokens, routes, norm_gain, router_weight)

    def pairs(move, back):
        places = [(e, target(e, move)) for e in range(experts)]
        return [(to, start) for start, to in places] if back else places

    def send(x, move, back=False):
        return x if move == (0, 0) else lax.ppermute(x, "expert", pairs(move, back))

    incoming = {move: send(x, move) for move, x in zip(moves, outgoing)}
    matrices = [gate_weight[0], up_weight[0], down_weight[0]]
    backs = []
    for at, group in enumerate(move_groups):
        results, matrices = expert_rows([incoming[move] for move in group], matrices, at == 0)
        backs += [send(x, move, back=True) for move, x in zip(group, results)]
    hidden_out, embedded, rounded = combine(tokens, slots, weights, backs, lengths)

    groups = lax.axis_size("dp")
    swap = [(i, i ^ 1) for i in range(groups)]
    colours = [[] for _ in range(2 * plane)]
    for device in range(groups * experts):
        dp, expert = divmod(device, experts)
        colours[(expert + 2 * (dp // line)) % plane * 2 + dp % 2].append(device)
    copies = jnp.broadcast_to(rounded[None], (len(colours[0]),) + rounded.shape)
    own = lax.all_to_all(
        copies, ("dp", "expert"), split_axis=0, concat_axis=0, tiled=True, axis_index_groups=colours
    )
    blocks = [
        own,
        lax.ppermute(own, "expert", pairs((3, 0), False)),
        lax.ppermute(own, "dp", [(i, (i - line) % groups) for i in range(groups)]),
        lax.ppermute(own, "expert", pairs((1, 0), False)),
    ]
    blocks += [lax.ppermute(x, "dp", swap) for x in blocks]
    half = rounded.shape[0] // 2
    queries = jnp.concatenate([x[:, :half] for x in blocks]).reshape(-1, width)
    docs = jnp.concatenate([x[:, half:] for x in blocks]).reshape(-1, width)
    query_grad, doc_grad = info_nce(queries, docs, embedded)
    return (hidden_out, query_grad, doc_grad)


def solution(mesh):
    placed = (
        P(("dp", "expert"), None),
        P(("dp", "expert"), None),
        P(("dp", "expert"), None),
        P(),
        P(),
        P("expert", None, None),
        P("expert", None, None),
        P("expert", None, None),
    )
    return jax.shard_map(
        body,
        mesh=mesh,
        in_specs=placed,
        out_specs=(P(("dp", "expert"), None), P(("dp", "expert"), None), P(("dp", "expert"), None)),
        check_vma=False,
    )
```

```python
import functools

import jax
import jax.numpy as jnp
from jax import lax
from jax.experimental import pallas as pl
from jax.experimental.pallas import tpu as pltpu
from jax.sharding import PartitionSpec as P

logit_scale = 50.0
norm_eps = 1e-06
pool_eps = 1e-06
f32 = jnp.float32
bf16 = jnp.bfloat16
mebibyte = 1024 * 1024
plane = 4
block = 512
head = 512
line = 4
move_groups = (
    ((0, 0), (1, 0), (3, 0), (0, 1)),
    ((2, 0), (1, 1)),
    ((3, 1), (2, 1)),
)
moves = [move for group in move_groups for move in group]


def dot(a, b):
    return jnp.dot(a, b, preferred_element_type=f32)


def dot_nt(a, b):
    return lax.dot_general(a, b, (((1,), (1,)), ((), ())), preferred_element_type=f32)


def target(expert, move):
    along, across = move
    return (expert // plane + across) % 2 * plane + (expert % plane + along) % plane


def iota(shape, axis):
    return lax.broadcasted_iota(jnp.int32, shape, axis)


def split(x):
    high = x.astype(bf16)
    return high, (x - high.astype(f32)).astype(bf16)


def fold(x):
    return x[: x.shape[0] // 2] + x[x.shape[0] // 2 :]


def call(kernel, outs, *operands, budget=16, outside=(), inside=(), **options):
    whole = pl.BlockSpec(memory_space=pltpu.VMEM)
    left = pl.BlockSpec(memory_space=pltpu.HBM)
    operands = [
        pltpu.with_memory_space_constraint(x, pltpu.HBM)
        if at in outside
        else pltpu.with_memory_space_constraint(x, pltpu.VMEM)
        if at in inside
        else x
        for at, x in enumerate(operands)
    ]
    return pl.pallas_call(
        kernel,
        out_shape=outs,
        in_specs=[left if at in outside else whole for at in range(len(operands))],
        out_specs=jax.tree.map(lambda _: whole, outs),
        compiler_params=pltpu.CompilerParams(vmem_limit_bytes=budget * mebibyte),
        **options,
    )(*operands)


def route_kernel(
    tokens_hbm, routes_hbm, gain_hbm, router_hbm, gate_hbm, up_hbm, *refs, head
):
    *out_refs, slots_ref, weights_ref, gate_ref, up_ref, tokens_ref, routes_ref, gain_ref, router_ref, sems = refs
    copies = [
        pltpu.make_async_copy(tokens_hbm, tokens_ref, sems.at[0]),
        pltpu.make_async_copy(gain_hbm, gain_ref, sems.at[1]),
        pltpu.make_async_copy(routes_hbm, routes_ref, sems.at[2]),
        pltpu.make_async_copy(router_hbm, router_ref, sems.at[3]),
    ]
    for copy in copies:
        copy.start()
    heads = [
        pltpu.make_async_copy(gate_hbm.at[:, :head], gate_ref.at[:, :head], sems.at[4]),
        pltpu.make_async_copy(up_hbm.at[:, :head], up_ref.at[:, :head], sems.at[5]),
    ]
    for copy in heads:
        copy.start()
    for copy in copies:
        copy.wait()
    rows = tokens_ref.shape[0]
    experts = router_ref.shape[0]
    capacity = out_refs[0].shape[0]
    here = lax.axis_index("expert")

    def ordered(shape):
        place, labels = iota(shape, 0), jnp.zeros(shape, jnp.int32)
        for at, move in enumerate(moves):
            labels = jnp.where(place == at, target(here, move), labels)
        return labels

    widened = tokens_ref[...].astype(f32)
    inverse = lax.rsqrt(jnp.mean(widened * widened, axis=-1, keepdims=True) + norm_eps)
    normed = (widened * inverse * gain_ref[...]).astype(bf16)
    labels = ordered((experts, rows))
    hit = (routes_ref[0:1, :] == labels) | (routes_ref[1:2, :] == labels)
    hits = jnp.where(hit, 1.0, 0.0).astype(bf16)
    down, across = iota((rows, rows), 0), iota((rows, rows), 1)
    ranks = dot(hits, jnp.where(down < across, 1.0, 0.0).astype(bf16))
    ranks = jnp.where(hit, ranks, -1.0)
    places = iota((capacity, rows), 0).astype(f32)
    for e in range(experts):
        chosen = jnp.where(places == ranks[e : e + 1, :], 1.0, 0.0).astype(bf16)
        out_refs[e][...] = dot(chosen, normed).astype(bf16)
    hits_down = dot_nt(jnp.where(down == across, 1.0, 0.0).astype(bf16), hits)
    ranks_down = dot_nt(jnp.where(across < down, 1.0, 0.0).astype(bf16), hits)
    picks = ordered((experts, experts)) == iota((experts, experts), 1)
    router = dot(jnp.where(picks, 1.0, 0.0).astype(bf16), router_ref[...]).astype(bf16)
    logits = dot_nt(normed, router)
    both = jnp.sum(hits_down * logits, axis=-1, keepdims=True)
    slots_ref[...] = jnp.where(hits_down > 0.5, ranks_down, -1.0)
    weights_ref[...] = hits_down / (1.0 + jnp.exp(both - 2.0 * logits))
    for copy in heads:
        copy.wait()


def stack(x_refs, x_ref):
    rows = x_refs[0].shape[0]
    for at, ref in enumerate(x_refs):
        x_ref[at * rows : (at + 1) * rows, :] = ref[...]


def unstack(x, out_refs):
    rows = out_refs[0].shape[0]
    for at, ref in enumerate(out_refs):
        ref[...] = x[at * rows : (at + 1) * rows, :]


def hidden_block(x_ref, gate_ref, up_ref, hidden_ref, at):
    x = x_ref[...]
    gate_act = dot(x, gate_ref[:, at])
    up_act = dot(x, up_ref[:, at])
    hidden_ref[:, at] = (gate_act / (1.0 + jnp.exp(-gate_act)) * up_act).astype(bf16)


def first_expert_kernel(*refs, blocks, block, present, ahead):
    x_refs, out_refs = refs[:blocks], refs[blocks + 5 : 2 * blocks + 5]
    gate_hbm, up_hbm, down_hbm = refs[blocks : blocks + 3]
    gate_ref, up_ref, down_ref, x_ref, hidden_ref, sems = refs[2 * blocks + 5 :]
    steps = hidden_ref.shape[1] // block

    def part(step):
        return pl.ds(pl.multiple_of(step * block, block), block)

    def fetches(step):
        at = part(step)
        return (
            pltpu.make_async_copy(gate_hbm.at[:, at], gate_ref.at[:, at], sems.at[0, step]),
            pltpu.make_async_copy(up_hbm.at[:, at], up_ref.at[:, at], sems.at[1, step]),
        )

    down_fetch = pltpu.make_async_copy(down_hbm, down_ref, sems.at[2, 0])
    for step in range(present, ahead):
        for copy in fetches(step):
            copy.start()
    stack(x_refs, x_ref)

    def columns(step, carry):
        @pl.when(step + ahead < steps)
        def _():
            for copy in fetches(step + ahead):
                copy.start()

        @pl.when(step + ahead == steps)
        def _():
            down_fetch.start()

        @pl.when(step >= present)
        def _():
            for copy in fetches(step):
                copy.wait()

        hidden_block(x_ref, gate_ref, up_ref, hidden_ref, part(step))
        return carry

    lax.fori_loop(0, steps, columns, 0)
    down_fetch.wait()
    unstack(dot(hidden_ref[...], down_ref[...]).astype(bf16), out_refs)


def later_expert_kernel(*refs, blocks, block):
    x_refs, out_refs = refs[:blocks], refs[blocks + 3 : 2 * blocks + 3]
    gate_ref, up_ref, down_ref = refs[blocks : blocks + 3]
    x_ref, hidden_ref = refs[2 * blocks + 3 :]
    stack(x_refs, x_ref)

    def columns(step, carry):
        at = pl.ds(pl.multiple_of(step * block, block), block)
        hidden_block(x_ref, gate_ref, up_ref, hidden_ref, at)
        return carry

    lax.fori_loop(0, hidden_ref.shape[1] // block, columns, 0)
    unstack(dot(hidden_ref[...], down_ref[...]).astype(bf16), out_refs)


def expert_rows(xs, weights, heads, ahead=2):
    rows, width = xs[0].shape
    hidden = weights[0].shape[1]
    blocks = len(xs)
    places = range(blocks, blocks + 3)
    results = [jax.ShapeDtypeStruct(x.shape, bf16) for x in xs]
    scratch = [pltpu.VMEM((blocks * rows, width), bf16), pltpu.VMEM((blocks * rows, hidden), bf16)]
    if heads:
        out = call(
            functools.partial(
                first_expert_kernel, blocks=blocks, block=block, present=head // block, ahead=ahead
            ),
            results + [jax.ShapeDtypeStruct(w.shape, bf16) for w in weights],
            *xs, *weights, *heads,
            budget=20,
            outside=places,
            inside=range(blocks + 3, blocks + 5),
            input_output_aliases={blocks + 3: blocks, blocks + 4: blocks + 1},
            scratch_shapes=scratch + [pltpu.SemaphoreType.DMA((3, hidden // block))],
        )
        return out[:blocks], out[blocks:]
    out = call(
        functools.partial(later_expert_kernel, blocks=blocks, block=block),
        results,
        *xs, *weights,
        budget=16,
        inside=places,
        scratch_shapes=scratch,
    )
    return out, weights


def weighted_rows(slots_ref, weights_ref, back_refs, start):
    shape = slots_ref.shape[0], back_refs[0].shape[0]
    lanes = iota(shape, 1).astype(f32)
    terms = [
        jnp.where(lanes == slots_ref[:, e : e + 1], weights_ref[:, e : e + 1], 0.0)
        for e in range(start, start + len(back_refs))
    ]
    high, low = split(jnp.concatenate(terms, axis=1))
    back = jnp.concatenate([ref[...] for ref in back_refs], axis=0)
    return dot(high, back) + dot(low, back)


def early_combine_kernel(tokens_ref, slots_ref, weights_ref, *refs):
    *back_refs, mixed_ref = refs
    mixed_ref[...] = tokens_ref[...].astype(f32) + weighted_rows(slots_ref, weights_ref, back_refs, 0)


def combine_kernel(early_ref, slots_ref, weights_ref, lengths_ref, *refs):
    *back_refs, hidden_ref, embedded_ref, rounded_ref = refs
    rows = early_ref.shape[0]
    start = slots_ref.shape[1] - len(back_refs)
    mixed = early_ref[...] + weighted_rows(slots_ref, weights_ref, back_refs, start)
    hidden_ref[...] = mixed.astype(bf16)
    count = lengths_ref.shape[1]
    spans = jnp.broadcast_to(lengths_ref[...], (count, count)).astype(f32)
    down, across = iota((count, count), 0), iota((count, count), 1)
    ends = jnp.sum(jnp.where(across <= down, spans, 0.0), axis=1, keepdims=True)
    sizes = jnp.sum(jnp.where(across == down, spans, 0.0), axis=1, keepdims=True)
    places = iota((count, rows), 1).astype(f32)
    member = jnp.where((places >= ends - sizes) & (places < ends), 1.0, 0.0).astype(bf16)
    first, rest = split(mixed)
    second, third = split(mixed - first.astype(f32))
    pooled = (dot(member, first) + dot(member, second) + dot(member, third)) / sizes
    embedded = pooled * lax.rsqrt(jnp.sum(pooled * pooled, axis=-1, keepdims=True) + pool_eps)
    embedded_ref[...] = embedded
    rounded_ref[...] = embedded.astype(bf16)


def gradient_kernel(queries_ref, docs_ref, embedded_ref, query_grad_ref, doc_grad_ref):
    rank = lax.axis_index("dp") // 2 * (lax.axis_size("expert") // plane) + lax.axis_index("expert") // plane
    first = rank * (embedded_ref.shape[0] // 2)
    embedded = embedded_ref[...]
    count = embedded.shape[0] // 2
    total = queries_ref.shape[0]
    queries, documents = embedded[:count], embedded[count:]
    all_queries, all_docs = queries_ref[...], docs_ref[...]
    block = 256
    sums = jnp.zeros((1, total), f32)
    for at in range(0, total, block):
        scores = dot_nt(docs_ref[at : at + block, :], all_queries)
        sums = sums + jnp.sum(jnp.exp(logit_scale * scores), axis=0, keepdims=True)
    stacked = jnp.concatenate(split(embedded), axis=0)
    rows = fold(dot_nt(stacked, all_docs))[:count]
    cols = fold(dot_nt(stacked, all_queries))[count:]
    own = iota((count, total), 1) == first + iota((count, total), 0)
    pair = jnp.exp(logit_scale * jnp.sum(queries * documents, axis=-1, keepdims=True))
    rows = jnp.where(own, 0.0, jnp.exp(logit_scale * rows))
    cols = jnp.where(own, 0.0, jnp.exp(logit_scale * cols))
    row_sum = jnp.sum(rows, axis=-1, keepdims=True) + pair
    diagonal = pair / row_sum - 1.0
    likely = jnp.concatenate([rows / row_sum, cols / sums], axis=0)
    likely = jnp.concatenate(split(likely), axis=0)
    query_grad_ref[...] = logit_scale * (fold(dot(likely, all_docs))[:count] + diagonal * documents)
    doc_grad_ref[...] = logit_scale * (fold(dot(likely, all_queries))[count:] + diagonal * queries)


def route(tokens, routes, norm_gain, router_weight, gate, up):
    rows, width = tokens.shape
    experts = router_weight.shape[1]
    operands = (tokens, routes.T, norm_gain, router_weight.T, gate, up)
    return call(
        functools.partial(route_kernel, head=head),
        [
            *[jax.ShapeDtypeStruct((rows // 2, width), bf16) for _ in range(experts)],
            jax.ShapeDtypeStruct((rows, experts), f32),
            jax.ShapeDtypeStruct((rows, experts), f32),
            jax.ShapeDtypeStruct(gate.shape, bf16),
            jax.ShapeDtypeStruct(up.shape, bf16),
        ],
        *operands,
        outside=range(6),
        scratch_shapes=[pltpu.VMEM(x.shape, x.dtype) for x in operands[:4]]
        + [pltpu.SemaphoreType.DMA((len(operands),))],
    )


def combine(tokens, slots, weights, backs, lengths):
    count, width = lengths.shape[1], tokens.shape[1]
    early = len(backs) - len(move_groups[-1])
    mixed = call(
        early_combine_kernel,
        jax.ShapeDtypeStruct(tokens.shape, f32),
        tokens, slots, weights, *backs[:early],
    )
    return call(
        combine_kernel,
        [
            jax.ShapeDtypeStruct(tokens.shape, bf16),
            jax.ShapeDtypeStruct((count, width), f32),
            jax.ShapeDtypeStruct((count, width), bf16),
        ],
        mixed, slots, weights, lengths, *backs[early:],
    )


def info_nce(queries, docs, embedded):
    out = jax.ShapeDtypeStruct((embedded.shape[0] // 2, embedded.shape[1]), f32)
    return call(gradient_kernel, [out, out], queries, docs, embedded)


def body(tokens, routes, lengths, norm_gain, router_weight, gate_weight, up_weight, down_weight):
    width = tokens.shape[1]
    experts = router_weight.shape[1]
    matrices = [gate_weight[0], up_weight[0], down_weight[0]]
    *outgoing, slots, weights, gate, up = route(
        tokens, routes, norm_gain, router_weight, *matrices[:2]
    )

    def pairs(move, back):
        places = [(e, target(e, move)) for e in range(experts)]
        return [(to, start) for start, to in places] if back else places

    def send(x, move, back=False):
        return x if move == (0, 0) else lax.ppermute(x, "expert", pairs(move, back))

    incoming = {move: send(x, move) for move, x in zip(moves, outgoing)}
    backs, heads = [], [gate, up]
    for group in move_groups:
        results, matrices = expert_rows([incoming[move] for move in group], matrices, heads)
        heads = []
        backs += [send(x, move, back=True) for move, x in zip(group, results)]
    hidden_out, embedded, rounded = combine(tokens, slots, weights, backs, lengths)

    groups = lax.axis_size("dp")
    swap = [(i, i ^ 1) for i in range(groups)]
    colours = [[] for _ in range(2 * plane)]
    for device in range(groups * experts):
        dp, expert = divmod(device, experts)
        colours[(expert + 2 * (dp // line)) % plane * 2 + dp % 2].append(device)
    copies = jnp.broadcast_to(rounded[None], (len(colours[0]),) + rounded.shape)
    own = lax.all_to_all(
        copies, ("dp", "expert"), split_axis=0, concat_axis=0, tiled=True, axis_index_groups=colours
    )
    blocks = [
        own,
        lax.ppermute(own, "expert", pairs((3, 0), False)),
        lax.ppermute(own, "dp", [(i, (i - line) % groups) for i in range(groups)]),
        lax.ppermute(own, "expert", pairs((1, 0), False)),
    ]
    blocks += [lax.ppermute(x, "dp", swap) for x in blocks]
    half = rounded.shape[0] // 2
    queries = jnp.concatenate([x[:, :half] for x in blocks]).reshape(-1, width)
    docs = jnp.concatenate([x[:, half:] for x in blocks]).reshape(-1, width)
    query_grad, doc_grad = info_nce(queries, docs, embedded)
    return (hidden_out, query_grad, doc_grad)


def solution(mesh):
    placed = (
        P(("dp", "expert"), None),
        P(("dp", "expert"), None),
        P(("dp", "expert"), None),
        P(),
        P(),
        P("expert", None, None),
        P("expert", None, None),
        P("expert", None, None),
    )
    return jax.shard_map(
        body,
        mesh=mesh,
        in_specs=placed,
        out_specs=(P(("dp", "expert"), None), P(("dp", "expert"), None), P(("dp", "expert"), None)),
        check_vma=False,
    )
```

```python
import functools

import jax
import jax.numpy as jnp
from jax import lax
from jax.experimental import pallas as pl
from jax.experimental.pallas import tpu as pltpu
from jax.sharding import PartitionSpec as P

logit_scale = 50.0
norm_eps = 1e-06
pool_eps = 1e-06
f32 = jnp.float32
bf16 = jnp.bfloat16
mebibyte = 1024 * 1024
plane = 4
block = 512
head = 512
line = 4
move_groups = (
    ((0, 0), (1, 0), (3, 0), (0, 1)),
    ((2, 0), (1, 1)),
    ((3, 1), (2, 1)),
)
moves = [move for group in move_groups for move in group]


def dot(a, b):
    return jnp.dot(a, b, preferred_element_type=f32)


def dot_nt(a, b):
    return lax.dot_general(a, b, (((1,), (1,)), ((), ())), preferred_element_type=f32)


def target(expert, move):
    along, across = move
    return (expert // plane + across) % 2 * plane + (expert % plane + along) % plane


def iota(shape, axis):
    return lax.broadcasted_iota(jnp.int32, shape, axis)


def split(x):
    high = x.astype(bf16)
    return high, (x - high.astype(f32)).astype(bf16)


def fold(x):
    return x[: x.shape[0] // 2] + x[x.shape[0] // 2 :]


def call(kernel, outs, *operands, budget=16, outside=(), inside=(), **options):
    whole = pl.BlockSpec(memory_space=pltpu.VMEM)
    left = pl.BlockSpec(memory_space=pltpu.HBM)
    operands = [
        pltpu.with_memory_space_constraint(x, pltpu.HBM)
        if at in outside
        else pltpu.with_memory_space_constraint(x, pltpu.VMEM)
        if at in inside
        else x
        for at, x in enumerate(operands)
    ]
    return pl.pallas_call(
        kernel,
        out_shape=outs,
        in_specs=[left if at in outside else whole for at in range(len(operands))],
        out_specs=jax.tree.map(lambda _: whole, outs),
        compiler_params=pltpu.CompilerParams(vmem_limit_bytes=budget * mebibyte),
        **options,
    )(*operands)


def route_kernel(
    tokens_hbm, routes_hbm, gain_hbm, router_hbm, gate_hbm, up_hbm, *refs, head
):
    *out_refs, slots_ref, weights_ref, gate_ref, up_ref, tokens_ref, routes_ref, gain_ref, router_ref, sems = refs
    copies = [
        pltpu.make_async_copy(tokens_hbm, tokens_ref, sems.at[0]),
        pltpu.make_async_copy(gain_hbm, gain_ref, sems.at[1]),
        pltpu.make_async_copy(routes_hbm, routes_ref, sems.at[2]),
        pltpu.make_async_copy(router_hbm, router_ref, sems.at[3]),
    ]
    for copy in copies:
        copy.start()
    heads = [
        pltpu.make_async_copy(gate_hbm.at[:, :head], gate_ref.at[:, :head], sems.at[4]),
        pltpu.make_async_copy(up_hbm.at[:, :head], up_ref.at[:, :head], sems.at[5]),
    ]
    for copy in heads:
        copy.start()
    for copy in copies:
        copy.wait()
    rows = tokens_ref.shape[0]
    experts = router_ref.shape[0]
    capacity = out_refs[0].shape[0]
    here = lax.axis_index("expert")

    def ordered(shape):
        place, labels = iota(shape, 0), jnp.zeros(shape, jnp.int32)
        for at, move in enumerate(moves):
            labels = jnp.where(place == at, target(here, move), labels)
        return labels

    widened = tokens_ref[...].astype(f32)
    inverse = lax.rsqrt(jnp.mean(widened * widened, axis=-1, keepdims=True) + norm_eps)
    normed = (widened * inverse * gain_ref[...]).astype(bf16)
    labels = ordered((experts, rows))
    hit = (routes_ref[0:1, :] == labels) | (routes_ref[1:2, :] == labels)
    hits = jnp.where(hit, 1.0, 0.0).astype(bf16)
    down, across = iota((rows, rows), 0), iota((rows, rows), 1)
    ranks = dot(hits, jnp.where(down < across, 1.0, 0.0).astype(bf16))
    ranks = jnp.where(hit, ranks, -1.0)
    places = iota((capacity, rows), 0).astype(f32)
    for e in range(experts):
        chosen = jnp.where(places == ranks[e : e + 1, :], 1.0, 0.0).astype(bf16)
        out_refs[e][...] = dot(chosen, normed).astype(bf16)
    hits_down = dot_nt(jnp.where(down == across, 1.0, 0.0).astype(bf16), hits)
    ranks_down = dot_nt(jnp.where(across < down, 1.0, 0.0).astype(bf16), hits)
    picks = ordered((experts, experts)) == iota((experts, experts), 1)
    router = dot(jnp.where(picks, 1.0, 0.0).astype(bf16), router_ref[...]).astype(bf16)
    logits = dot_nt(normed, router)
    both = jnp.sum(hits_down * logits, axis=-1, keepdims=True)
    slots_ref[...] = jnp.where(hits_down > 0.5, ranks_down, -1.0)
    weights_ref[...] = hits_down / (1.0 + jnp.exp(both - 2.0 * logits))
    for copy in heads:
        copy.wait()


def stack(x_refs, x_ref):
    rows = x_refs[0].shape[0]
    for at, ref in enumerate(x_refs):
        x_ref[at * rows : (at + 1) * rows, :] = ref[...]


def unstack(x, out_refs):
    rows = out_refs[0].shape[0]
    for at, ref in enumerate(out_refs):
        ref[...] = x[at * rows : (at + 1) * rows, :]


def hidden_block(x_ref, gate_ref, up_ref, hidden_ref, at):
    x = x_ref[...]
    gate_act = dot(x, gate_ref[:, at])
    up_act = dot(x, up_ref[:, at])
    hidden_ref[:, at] = (gate_act / (1.0 + jnp.exp(-gate_act)) * up_act).astype(bf16)


def first_expert_kernel(*refs, blocks, held, block, present, ahead):
    outs = blocks + 5 + held
    x_refs, out_refs = refs[:blocks], refs[outs : outs + blocks]
    gate_hbm, up_hbm, down_hbm = refs[blocks : blocks + 3]
    gate_ref, up_ref, down_ref = refs[outs + blocks : outs + blocks + 3]
    x_ref, hidden_ref, sems = refs[outs + blocks + 3 + held :]
    steps = hidden_ref.shape[1] // block

    def part(step):
        return pl.ds(pl.multiple_of(step * block, block), block)

    def fetches(step):
        at = part(step)
        return (
            pltpu.make_async_copy(gate_hbm.at[:, at], gate_ref.at[:, at], sems.at[0, step]),
            pltpu.make_async_copy(up_hbm.at[:, at], up_ref.at[:, at], sems.at[1, step]),
        )

    down_fetch = pltpu.make_async_copy(down_hbm, down_ref, sems.at[2, 0])
    for step in range(present, ahead):
        for copy in fetches(step):
            copy.start()
    stack(x_refs, x_ref)

    def columns(step, carry):
        @pl.when(step + ahead < steps)
        def _():
            for copy in fetches(step + ahead):
                copy.start()

        @pl.when(step + ahead == steps)
        def _():
            down_fetch.start()

        @pl.when(step >= present)
        def _():
            for copy in fetches(step):
                copy.wait()

        hidden_block(x_ref, gate_ref, up_ref, hidden_ref, part(step))
        return carry

    lax.fori_loop(0, steps, columns, 0)
    down_fetch.wait()
    unstack(dot(hidden_ref[...], down_ref[...]).astype(bf16), out_refs)


def later_expert_kernel(*refs, blocks, block):
    x_refs, out_refs = refs[:blocks], refs[blocks + 3 : 2 * blocks + 3]
    gate_ref, up_ref, down_ref = refs[blocks : blocks + 3]
    x_ref, hidden_ref = refs[2 * blocks + 3 :]
    stack(x_refs, x_ref)

    def columns(step, carry):
        at = pl.ds(pl.multiple_of(step * block, block), block)
        hidden_block(x_ref, gate_ref, up_ref, hidden_ref, at)
        return carry

    lax.fori_loop(0, hidden_ref.shape[1] // block, columns, 0)
    unstack(dot(hidden_ref[...], down_ref[...]).astype(bf16), out_refs)


def expert_rows(xs, weights, heads, held, ahead=2):
    rows, width = xs[0].shape
    hidden = weights[0].shape[1]
    blocks = len(xs)
    places = range(blocks, blocks + 3)
    results = [jax.ShapeDtypeStruct(x.shape, bf16) for x in xs]
    scratch = [pltpu.VMEM((blocks * rows, width), bf16), pltpu.VMEM((blocks * rows, hidden), bf16)]
    if heads:
        out = call(
            functools.partial(
                first_expert_kernel,
                blocks=blocks,
                held=len(held),
                block=block,
                present=head // block,
                ahead=ahead,
            ),
            results + [jax.ShapeDtypeStruct(w.shape, bf16) for w in [*weights, *held]],
            *xs, *weights, *heads, *held,
            budget=20,
            outside=places,
            inside=range(blocks + 3, blocks + 5),
            input_output_aliases={
                blocks + 3: blocks,
                blocks + 4: blocks + 1,
                **{blocks + 5 + at: blocks + 3 + at for at in range(len(held))},
            },
            scratch_shapes=scratch + [pltpu.SemaphoreType.DMA((3, hidden // block))],
        )
        return out[:blocks], out[blocks : blocks + 3], out[blocks + 3 :]
    out = call(
        functools.partial(later_expert_kernel, blocks=blocks, block=block),
        results,
        *xs, *weights,
        budget=16,
        inside=places,
        scratch_shapes=scratch,
    )
    return out, weights, held


def weighted_rows(slots_ref, weights_ref, back_refs, start):
    shape = slots_ref.shape[0], back_refs[0].shape[0]
    lanes = iota(shape, 1).astype(f32)
    terms = [
        jnp.where(lanes == slots_ref[:, e : e + 1], weights_ref[:, e : e + 1], 0.0)
        for e in range(start, start + len(back_refs))
    ]
    high, low = split(jnp.concatenate(terms, axis=1))
    back = jnp.concatenate([ref[...] for ref in back_refs], axis=0)
    return dot(high, back) + dot(low, back)


def early_combine_kernel(tokens_ref, slots_ref, weights_ref, *refs):
    *back_refs, mixed_ref = refs
    mixed_ref[...] = tokens_ref[...].astype(f32) + weighted_rows(slots_ref, weights_ref, back_refs, 0)


def combine_kernel(early_ref, slots_ref, weights_ref, lengths_ref, *refs):
    *back_refs, hidden_ref, embedded_ref, rounded_ref = refs
    rows = early_ref.shape[0]
    start = slots_ref.shape[1] - len(back_refs)
    mixed = early_ref[...] + weighted_rows(slots_ref, weights_ref, back_refs, start)
    hidden_ref[...] = mixed.astype(bf16)
    count = lengths_ref.shape[1]
    spans = jnp.broadcast_to(lengths_ref[...], (count, count)).astype(f32)
    down, across = iota((count, count), 0), iota((count, count), 1)
    ends = jnp.sum(jnp.where(across <= down, spans, 0.0), axis=1, keepdims=True)
    sizes = jnp.sum(jnp.where(across == down, spans, 0.0), axis=1, keepdims=True)
    places = iota((count, rows), 1).astype(f32)
    member = jnp.where((places >= ends - sizes) & (places < ends), 1.0, 0.0).astype(bf16)
    first, rest = split(mixed)
    second, third = split(mixed - first.astype(f32))
    pooled = (dot(member, first) + dot(member, second) + dot(member, third)) / sizes
    embedded = pooled * lax.rsqrt(jnp.sum(pooled * pooled, axis=-1, keepdims=True) + pool_eps)
    embedded_ref[...] = embedded
    rounded_ref[...] = embedded.astype(bf16)


def gradient_kernel(queries_ref, docs_ref, embedded_ref, query_grad_ref, doc_grad_ref):
    rank = lax.axis_index("dp") // 2 * (lax.axis_size("expert") // plane) + lax.axis_index("expert") // plane
    first = rank * (embedded_ref.shape[0] // 2)
    embedded = embedded_ref[...]
    count = embedded.shape[0] // 2
    total = queries_ref.shape[0]
    queries, documents = embedded[:count], embedded[count:]
    all_queries, all_docs = queries_ref[...], docs_ref[...]
    block = 256
    sums = jnp.zeros((1, total), f32)
    for at in range(0, total, block):
        scores = dot_nt(docs_ref[at : at + block, :], all_queries)
        sums = sums + jnp.sum(jnp.exp(logit_scale * scores), axis=0, keepdims=True)
    stacked = jnp.concatenate(split(embedded), axis=0)
    rows = fold(dot_nt(stacked, all_docs))[:count]
    cols = fold(dot_nt(stacked, all_queries))[count:]
    own = iota((count, total), 1) == first + iota((count, total), 0)
    pair = jnp.exp(logit_scale * jnp.sum(queries * documents, axis=-1, keepdims=True))
    rows = jnp.where(own, 0.0, jnp.exp(logit_scale * rows))
    cols = jnp.where(own, 0.0, jnp.exp(logit_scale * cols))
    row_sum = jnp.sum(rows, axis=-1, keepdims=True) + pair
    diagonal = pair / row_sum - 1.0
    likely = jnp.concatenate([rows / row_sum, cols / sums], axis=0)
    likely = jnp.concatenate(split(likely), axis=0)
    query_grad_ref[...] = logit_scale * (fold(dot(likely, all_docs))[:count] + diagonal * documents)
    doc_grad_ref[...] = logit_scale * (fold(dot(likely, all_queries))[count:] + diagonal * queries)


def route(tokens, routes, norm_gain, router_weight, gate, up):
    rows, width = tokens.shape
    experts = router_weight.shape[1]
    operands = (tokens, routes.T, norm_gain, router_weight.T, gate, up)
    return call(
        functools.partial(route_kernel, head=head),
        [
            *[jax.ShapeDtypeStruct((rows // 2, width), bf16) for _ in range(experts)],
            jax.ShapeDtypeStruct((rows, experts), f32),
            jax.ShapeDtypeStruct((rows, experts), f32),
            jax.ShapeDtypeStruct(gate.shape, bf16),
            jax.ShapeDtypeStruct(up.shape, bf16),
        ],
        *operands,
        outside=range(6),
        scratch_shapes=[pltpu.VMEM(x.shape, x.dtype) for x in operands[:4]]
        + [pltpu.SemaphoreType.DMA((len(operands),))],
    )


def combine(tokens, slots, weights, backs, lengths):
    count, width = lengths.shape[1], tokens.shape[1]
    early = len(backs) - len(move_groups[-1])
    mixed = call(
        early_combine_kernel,
        jax.ShapeDtypeStruct(tokens.shape, f32),
        tokens, slots, weights, *backs[:early],
    )
    return call(
        combine_kernel,
        [
            jax.ShapeDtypeStruct(tokens.shape, bf16),
            jax.ShapeDtypeStruct((count, width), f32),
            jax.ShapeDtypeStruct((count, width), bf16),
        ],
        mixed, slots, weights, lengths, *backs[early:],
    )


def info_nce(queries, docs, embedded):
    out = jax.ShapeDtypeStruct((embedded.shape[0] // 2, embedded.shape[1]), f32)
    return call(gradient_kernel, [out, out], queries, docs, embedded)


def body(tokens, routes, lengths, norm_gain, router_weight, gate_weight, up_weight, down_weight):
    width = tokens.shape[1]
    experts = router_weight.shape[1]
    matrices = [gate_weight[0], up_weight[0], down_weight[0]]
    *outgoing, slots, weights, gate, up = route(
        tokens, routes, norm_gain, router_weight, *matrices[:2]
    )

    def pairs(move, back):
        places = [(e, target(e, move)) for e in range(experts)]
        return [(to, start) for start, to in places] if back else places

    def send(x, move, back=False):
        return x if move == (0, 0) else lax.ppermute(x, "expert", pairs(move, back))

    late = move_groups[-1]
    held = outgoing[-len(late) :]
    incoming = {move: send(x, move) for move, x in zip(moves, outgoing) if move not in late}
    backs, heads = [], [gate, up]
    for group in move_groups:
        results, matrices, held = expert_rows(
            [incoming[move] for move in group], matrices, heads, held
        )
        if heads:
            incoming |= {move: send(x, move) for move, x in zip(late, held)}
        heads = []
        backs += [send(x, move, back=True) for move, x in zip(group, results)]
    hidden_out, embedded, rounded = combine(tokens, slots, weights, backs, lengths)

    groups = lax.axis_size("dp")
    swap = [(i, i ^ 1) for i in range(groups)]
    colours = [[] for _ in range(2 * plane)]
    for device in range(groups * experts):
        dp, expert = divmod(device, experts)
        colours[(expert + 2 * (dp // line)) % plane * 2 + dp % 2].append(device)
    copies = jnp.broadcast_to(rounded[None], (len(colours[0]),) + rounded.shape)
    own = lax.all_to_all(
        copies, ("dp", "expert"), split_axis=0, concat_axis=0, tiled=True, axis_index_groups=colours
    )
    blocks = [
        own,
        lax.ppermute(own, "expert", pairs((3, 0), False)),
        lax.ppermute(own, "dp", [(i, (i - line) % groups) for i in range(groups)]),
        lax.ppermute(own, "expert", pairs((1, 0), False)),
    ]
    blocks += [lax.ppermute(x, "dp", swap) for x in blocks]
    half = rounded.shape[0] // 2
    queries = jnp.concatenate([x[:, :half] for x in blocks]).reshape(-1, width)
    docs = jnp.concatenate([x[:, half:] for x in blocks]).reshape(-1, width)
    query_grad, doc_grad = info_nce(queries, docs, embedded)
    return (hidden_out, query_grad, doc_grad)


def solution(mesh):
    placed = (
        P(("dp", "expert"), None),
        P(("dp", "expert"), None),
        P(("dp", "expert"), None),
        P(),
        P(),
        P("expert", None, None),
        P("expert", None, None),
        P("expert", None, None),
    )
    return jax.shard_map(
        body,
        mesh=mesh,
        in_specs=placed,
        out_specs=(P(("dp", "expert"), None), P(("dp", "expert"), None), P(("dp", "expert"), None)),
        check_vma=False,
    )
```

```python
import functools

import jax
import jax.numpy as jnp
from jax import lax
from jax.experimental import pallas as pl
from jax.experimental.pallas import tpu as pltpu
from jax.sharding import PartitionSpec as P

logit_scale = 50.0
norm_eps = 1e-06
pool_eps = 1e-06
f32 = jnp.float32
bf16 = jnp.bfloat16
mebibyte = 1024 * 1024
plane = 4
block = 512
head = 512
line = 4
move_groups = (
    ((0, 0), (1, 0), (3, 0), (0, 1)),
    ((2, 0), (1, 1)),
    ((3, 1), (2, 1)),
)
moves = [move for group in move_groups for move in group]


def dot(a, b):
    return jnp.dot(a, b, preferred_element_type=f32)


def dot_nt(a, b):
    return lax.dot_general(a, b, (((1,), (1,)), ((), ())), preferred_element_type=f32)


def target(expert, move):
    along, across = move
    return (expert // plane + across) % 2 * plane + (expert % plane + along) % plane


def iota(shape, axis):
    return lax.broadcasted_iota(jnp.int32, shape, axis)


def split(x):
    high = x.astype(bf16)
    return high, (x - high.astype(f32)).astype(bf16)


def fold(x):
    return x[: x.shape[0] // 2] + x[x.shape[0] // 2 :]


def call(kernel, outs, *operands, budget=16, outside=(), inside=(), **options):
    whole = pl.BlockSpec(memory_space=pltpu.VMEM)
    left = pl.BlockSpec(memory_space=pltpu.HBM)
    operands = [
        pltpu.with_memory_space_constraint(x, pltpu.HBM)
        if at in outside
        else pltpu.with_memory_space_constraint(x, pltpu.VMEM)
        if at in inside
        else x
        for at, x in enumerate(operands)
    ]
    return pl.pallas_call(
        kernel,
        out_shape=outs,
        in_specs=[left if at in outside else whole for at in range(len(operands))],
        out_specs=jax.tree.map(lambda _: whole, outs),
        compiler_params=pltpu.CompilerParams(vmem_limit_bytes=budget * mebibyte),
        **options,
    )(*operands)


def route_kernel(
    tokens_hbm, routes_hbm, gain_hbm, router_hbm, gate_hbm, up_hbm, *refs, head
):
    *out_refs, slots_ref, weights_ref, gate_ref, up_ref, tokens_ref, routes_ref, gain_ref, router_ref, sems = refs
    copies = [
        pltpu.make_async_copy(tokens_hbm, tokens_ref, sems.at[0]),
        pltpu.make_async_copy(gain_hbm, gain_ref, sems.at[1]),
        pltpu.make_async_copy(routes_hbm, routes_ref, sems.at[2]),
        pltpu.make_async_copy(router_hbm, router_ref, sems.at[3]),
    ]
    for copy in copies:
        copy.start()
    heads = [
        pltpu.make_async_copy(gate_hbm.at[:, :head], gate_ref.at[:, :head], sems.at[4]),
        pltpu.make_async_copy(up_hbm.at[:, :head], up_ref.at[:, :head], sems.at[5]),
    ]
    for copy in heads:
        copy.start()
    for copy in copies:
        copy.wait()
    rows = tokens_ref.shape[0]
    experts = router_ref.shape[0]
    capacity = out_refs[0].shape[0]
    here = lax.axis_index("expert")

    def ordered(shape):
        place, labels = iota(shape, 0), jnp.zeros(shape, jnp.int32)
        for at, move in enumerate(moves):
            labels = jnp.where(place == at, target(here, move), labels)
        return labels

    widened = tokens_ref[...].astype(f32)
    inverse = lax.rsqrt(jnp.mean(widened * widened, axis=-1, keepdims=True) + norm_eps)
    normed = (widened * inverse * gain_ref[...]).astype(bf16)
    labels = ordered((experts, rows))
    hit = (routes_ref[0:1, :] == labels) | (routes_ref[1:2, :] == labels)
    hits = jnp.where(hit, 1.0, 0.0).astype(bf16)
    down, across = iota((rows, rows), 0), iota((rows, rows), 1)
    ranks = dot(hits, jnp.where(down < across, 1.0, 0.0).astype(bf16))
    ranks = jnp.where(hit, ranks, -1.0)
    places = iota((capacity, rows), 0).astype(f32)
    for e in range(experts):
        chosen = jnp.where(places == ranks[e : e + 1, :], 1.0, 0.0).astype(bf16)
        out_refs[e][...] = dot(chosen, normed).astype(bf16)
    hits_down = dot_nt(jnp.where(down == across, 1.0, 0.0).astype(bf16), hits)
    ranks_down = dot_nt(jnp.where(across < down, 1.0, 0.0).astype(bf16), hits)
    picks = ordered((experts, experts)) == iota((experts, experts), 1)
    router = dot(jnp.where(picks, 1.0, 0.0).astype(bf16), router_ref[...]).astype(bf16)
    logits = dot_nt(normed, router)
    both = jnp.sum(hits_down * logits, axis=-1, keepdims=True)
    slots_ref[...] = jnp.where(hits_down > 0.5, ranks_down, -1.0)
    weights_ref[...] = hits_down / (1.0 + jnp.exp(both - 2.0 * logits))
    for copy in heads:
        copy.wait()


def stack(x_refs, x_ref):
    rows = x_refs[0].shape[0]
    for at, ref in enumerate(x_refs):
        x_ref[at * rows : (at + 1) * rows, :] = ref[...]


def unstack(x, out_refs):
    rows = out_refs[0].shape[0]
    for at, ref in enumerate(out_refs):
        ref[...] = x[at * rows : (at + 1) * rows, :]


def hidden_block(x_ref, gate_ref, up_ref, hidden_ref, at):
    x = x_ref[...]
    gate_act = dot(x, gate_ref[:, at])
    up_act = dot(x, up_ref[:, at])
    hidden_ref[:, at] = (gate_act / (1.0 + jnp.exp(-gate_act)) * up_act).astype(bf16)


def first_expert_kernel(*refs, blocks, block, present, ahead):
    x_refs, out_refs = refs[:blocks], refs[blocks + 5 : 2 * blocks + 5]
    gate_hbm, up_hbm, down_hbm = refs[blocks : blocks + 3]
    gate_ref, up_ref, down_ref, x_ref, hidden_ref, sems = refs[2 * blocks + 5 :]
    steps = hidden_ref.shape[1] // block

    def part(step):
        return pl.ds(pl.multiple_of(step * block, block), block)

    def fetches(step):
        at = part(step)
        return (
            pltpu.make_async_copy(gate_hbm.at[:, at], gate_ref.at[:, at], sems.at[0, step]),
            pltpu.make_async_copy(up_hbm.at[:, at], up_ref.at[:, at], sems.at[1, step]),
        )

    down_fetch = pltpu.make_async_copy(down_hbm, down_ref, sems.at[2, 0])
    for step in range(present, ahead):
        for copy in fetches(step):
            copy.start()
    stack(x_refs, x_ref)

    def columns(step, carry):
        @pl.when(step + ahead < steps)
        def _():
            for copy in fetches(step + ahead):
                copy.start()

        @pl.when(step + ahead == steps)
        def _():
            down_fetch.start()

        @pl.when(step >= present)
        def _():
            for copy in fetches(step):
                copy.wait()

        hidden_block(x_ref, gate_ref, up_ref, hidden_ref, part(step))
        return carry

    lax.fori_loop(0, steps, columns, 0)
    down_fetch.wait()
    unstack(dot(hidden_ref[...], down_ref[...]).astype(bf16), out_refs)


def later_expert_kernel(*refs, blocks, block):
    x_refs, out_refs = refs[:blocks], refs[blocks + 3 : 2 * blocks + 3]
    gate_ref, up_ref, down_ref = refs[blocks : blocks + 3]
    x_ref, hidden_ref = refs[2 * blocks + 3 :]
    stack(x_refs, x_ref)

    def columns(step, carry):
        at = pl.ds(pl.multiple_of(step * block, block), block)
        hidden_block(x_ref, gate_ref, up_ref, hidden_ref, at)
        return carry

    lax.fori_loop(0, hidden_ref.shape[1] // block, columns, 0)
    unstack(dot(hidden_ref[...], down_ref[...]).astype(bf16), out_refs)


def expert_rows(xs, weights, heads, ahead=2):
    rows, width = xs[0].shape
    hidden = weights[0].shape[1]
    blocks = len(xs)
    places = range(blocks, blocks + 3)
    results = [jax.ShapeDtypeStruct(x.shape, bf16) for x in xs]
    scratch = [pltpu.VMEM((blocks * rows, width), bf16), pltpu.VMEM((blocks * rows, hidden), bf16)]
    if heads:
        out = call(
            functools.partial(
                first_expert_kernel, blocks=blocks, block=block, present=head // block, ahead=ahead
            ),
            results + [jax.ShapeDtypeStruct(w.shape, bf16) for w in weights],
            *xs, *weights, *heads,
            budget=20,
            outside=places,
            inside=range(blocks + 3, blocks + 5),
            input_output_aliases={blocks + 3: blocks, blocks + 4: blocks + 1},
            scratch_shapes=scratch + [pltpu.SemaphoreType.DMA((3, hidden // block))],
        )
        return out[:blocks], out[blocks:]
    out = call(
        functools.partial(later_expert_kernel, blocks=blocks, block=block),
        results,
        *xs, *weights,
        budget=16,
        inside=places,
        scratch_shapes=scratch,
    )
    return out, weights


def weighted_rows(slots_ref, weights_ref, back_refs, start):
    shape = slots_ref.shape[0], back_refs[0].shape[0]
    lanes = iota(shape, 1).astype(f32)
    terms = [
        jnp.where(lanes == slots_ref[:, e : e + 1], weights_ref[:, e : e + 1], 0.0)
        for e in range(start, start + len(back_refs))
    ]
    high, low = split(jnp.concatenate(terms, axis=1))
    back = jnp.concatenate([ref[...] for ref in back_refs], axis=0)
    return dot(high, back) + dot(low, back)


def early_combine_kernel(tokens_ref, slots_ref, weights_ref, *refs):
    *back_refs, mixed_ref = refs
    mixed_ref[...] = tokens_ref[...].astype(f32) + weighted_rows(slots_ref, weights_ref, back_refs, 0)


def combine_kernel(early_ref, slots_ref, weights_ref, lengths_ref, *refs):
    *back_refs, mixed_ref, embedded_ref, rounded_ref = refs
    rows = early_ref.shape[0]
    start = slots_ref.shape[1] - len(back_refs)
    mixed = early_ref[...] + weighted_rows(slots_ref, weights_ref, back_refs, start)
    mixed_ref[...] = mixed
    count = lengths_ref.shape[1]
    spans = jnp.broadcast_to(lengths_ref[...], (count, count)).astype(f32)
    down, across = iota((count, count), 0), iota((count, count), 1)
    ends = jnp.sum(jnp.where(across <= down, spans, 0.0), axis=1, keepdims=True)
    sizes = jnp.sum(jnp.where(across == down, spans, 0.0), axis=1, keepdims=True)
    places = iota((count, rows), 1).astype(f32)
    member = jnp.where((places >= ends - sizes) & (places < ends), 1.0, 0.0).astype(bf16)
    first, rest = split(mixed)
    second, third = split(mixed - first.astype(f32))
    pooled = (dot(member, first) + dot(member, second) + dot(member, third)) / sizes
    embedded = pooled * lax.rsqrt(jnp.sum(pooled * pooled, axis=-1, keepdims=True) + pool_eps)
    embedded_ref[...] = embedded
    rounded_ref[...] = embedded.astype(bf16)


def gradient_kernel(queries_ref, docs_ref, embedded_ref, query_grad_ref, doc_grad_ref):
    rank = lax.axis_index("dp") // 2 * (lax.axis_size("expert") // plane) + lax.axis_index("expert") // plane
    first = rank * (embedded_ref.shape[0] // 2)
    embedded = embedded_ref[...]
    count = embedded.shape[0] // 2
    total = queries_ref.shape[0]
    queries, documents = embedded[:count], embedded[count:]
    all_queries, all_docs = queries_ref[...], docs_ref[...]
    block = 256
    sums = jnp.zeros((1, total), f32)
    for at in range(0, total, block):
        scores = dot_nt(docs_ref[at : at + block, :], all_queries)
        sums = sums + jnp.sum(jnp.exp(logit_scale * scores), axis=0, keepdims=True)
    stacked = jnp.concatenate(split(embedded), axis=0)
    rows = fold(dot_nt(stacked, all_docs))[:count]
    cols = fold(dot_nt(stacked, all_queries))[count:]
    own = iota((count, total), 1) == first + iota((count, total), 0)
    pair = jnp.exp(logit_scale * jnp.sum(queries * documents, axis=-1, keepdims=True))
    rows = jnp.where(own, 0.0, jnp.exp(logit_scale * rows))
    cols = jnp.where(own, 0.0, jnp.exp(logit_scale * cols))
    row_sum = jnp.sum(rows, axis=-1, keepdims=True) + pair
    diagonal = pair / row_sum - 1.0
    likely = jnp.concatenate([rows / row_sum, cols / sums], axis=0)
    likely = jnp.concatenate(split(likely), axis=0)
    query_grad_ref[...] = logit_scale * (fold(dot(likely, all_docs))[:count] + diagonal * documents)
    doc_grad_ref[...] = logit_scale * (fold(dot(likely, all_queries))[count:] + diagonal * queries)


def route(tokens, routes, norm_gain, router_weight, gate, up):
    rows, width = tokens.shape
    experts = router_weight.shape[1]
    operands = (tokens, routes.T, norm_gain, router_weight.T, gate, up)
    return call(
        functools.partial(route_kernel, head=head),
        [
            *[jax.ShapeDtypeStruct((rows // 2, width), bf16) for _ in range(experts)],
            jax.ShapeDtypeStruct((rows, experts), f32),
            jax.ShapeDtypeStruct((rows, experts), f32),
            jax.ShapeDtypeStruct(gate.shape, bf16),
            jax.ShapeDtypeStruct(up.shape, bf16),
        ],
        *operands,
        outside=range(6),
        scratch_shapes=[pltpu.VMEM(x.shape, x.dtype) for x in operands[:4]]
        + [pltpu.SemaphoreType.DMA((len(operands),))],
    )


def combine(tokens, slots, weights, backs, lengths):
    count, width = lengths.shape[1], tokens.shape[1]
    early = len(backs) - len(move_groups[-1])
    mixed = call(
        early_combine_kernel,
        jax.ShapeDtypeStruct(tokens.shape, f32),
        tokens, slots, weights, *backs[:early],
    )
    return call(
        combine_kernel,
        [
            jax.ShapeDtypeStruct(tokens.shape, f32),
            jax.ShapeDtypeStruct((count, width), f32),
            jax.ShapeDtypeStruct((count, width), bf16),
        ],
        mixed, slots, weights, lengths, *backs[early:],
    )


def info_nce(queries, docs, embedded):
    out = jax.ShapeDtypeStruct((embedded.shape[0] // 2, embedded.shape[1]), f32)
    return call(gradient_kernel, [out, out], queries, docs, embedded)


def body(tokens, routes, lengths, norm_gain, router_weight, gate_weight, up_weight, down_weight):
    width = tokens.shape[1]
    experts = router_weight.shape[1]
    matrices = [gate_weight[0], up_weight[0], down_weight[0]]
    *outgoing, slots, weights, gate, up = route(
        tokens, routes, norm_gain, router_weight, *matrices[:2]
    )

    def pairs(move, back):
        places = [(e, target(e, move)) for e in range(experts)]
        return [(to, start) for start, to in places] if back else places

    def send(x, move, back=False):
        return x if move == (0, 0) else lax.ppermute(x, "expert", pairs(move, back))

    incoming = {move: send(x, move) for move, x in zip(moves, outgoing)}
    backs, heads = [], [gate, up]
    for group in move_groups:
        results, matrices = expert_rows([incoming[move] for move in group], matrices, heads)
        heads = []
        backs += [send(x, move, back=True) for move, x in zip(group, results)]
    mixed, embedded, rounded = combine(tokens, slots, weights, backs, lengths)

    groups = lax.axis_size("dp")
    swap = [(i, i ^ 1) for i in range(groups)]
    colours = [[] for _ in range(2 * plane)]
    for device in range(groups * experts):
        dp, expert = divmod(device, experts)
        colours[(expert + 2 * (dp // line)) % plane * 2 + dp % 2].append(device)
    copies = jnp.broadcast_to(rounded[None], (len(colours[0]),) + rounded.shape)
    own = lax.all_to_all(
        copies, ("dp", "expert"), split_axis=0, concat_axis=0, tiled=True, axis_index_groups=colours
    )
    blocks = [
        own,
        lax.ppermute(own, "expert", pairs((3, 0), False)),
        lax.ppermute(own, "dp", [(i, (i - line) % groups) for i in range(groups)]),
        lax.ppermute(own, "expert", pairs((1, 0), False)),
    ]
    blocks += [lax.ppermute(x, "dp", swap) for x in blocks]
    half = rounded.shape[0] // 2
    queries = jnp.concatenate([x[:, :half] for x in blocks]).reshape(-1, width)
    docs = jnp.concatenate([x[:, half:] for x in blocks]).reshape(-1, width)
    query_grad, doc_grad = info_nce(queries, docs, embedded)
    return (mixed.astype(bf16), query_grad, doc_grad)


def solution(mesh):
    placed = (
        P(("dp", "expert"), None),
        P(("dp", "expert"), None),
        P(("dp", "expert"), None),
        P(),
        P(),
        P("expert", None, None),
        P("expert", None, None),
        P("expert", None, None),
    )
    return jax.shard_map(
        body,
        mesh=mesh,
        in_specs=placed,
        out_specs=(P(("dp", "expert"), None), P(("dp", "expert"), None), P(("dp", "expert"), None)),
        check_vma=False,
    )
```

```python
import functools

import jax
import jax.numpy as jnp
from jax import lax
from jax.experimental import pallas as pl
from jax.experimental.pallas import tpu as pltpu
from jax.sharding import PartitionSpec as P

logit_scale = 50.0
norm_eps = 1e-06
pool_eps = 1e-06
f32 = jnp.float32
bf16 = jnp.bfloat16
mebibyte = 1024 * 1024
plane = 4
block = 512
head = 512
line = 4
move_groups = (
    ((0, 0), (1, 0), (3, 0), (0, 1)),
    ((2, 0), (1, 1)),
    ((3, 1), (2, 1)),
)
moves = [move for group in move_groups for move in group]


def dot(a, b):
    return jnp.dot(a, b, preferred_element_type=f32)


def dot_nt(a, b):
    return lax.dot_general(a, b, (((1,), (1,)), ((), ())), preferred_element_type=f32)


def target(expert, move):
    along, across = move
    return (expert // plane + across) % 2 * plane + (expert % plane + along) % plane


def iota(shape, axis):
    return lax.broadcasted_iota(jnp.int32, shape, axis)


def split(x):
    high = x.astype(bf16)
    return high, (x - high.astype(f32)).astype(bf16)


def fold(x):
    return x[: x.shape[0] // 2] + x[x.shape[0] // 2 :]


def call(kernel, outs, *operands, budget=16, outside=(), inside=(), **options):
    whole = pl.BlockSpec(memory_space=pltpu.VMEM)
    left = pl.BlockSpec(memory_space=pltpu.HBM)
    operands = [
        pltpu.with_memory_space_constraint(x, pltpu.HBM)
        if at in outside
        else pltpu.with_memory_space_constraint(x, pltpu.VMEM)
        if at in inside
        else x
        for at, x in enumerate(operands)
    ]
    return pl.pallas_call(
        kernel,
        out_shape=outs,
        in_specs=[left if at in outside else whole for at in range(len(operands))],
        out_specs=jax.tree.map(lambda _: whole, outs),
        compiler_params=pltpu.CompilerParams(vmem_limit_bytes=budget * mebibyte),
        **options,
    )(*operands)


def route_kernel(
    tokens_hbm, routes_hbm, gain_hbm, router_hbm, gate_hbm, up_hbm, *refs, head
):
    *out_refs, slots_ref, weights_ref, gate_ref, up_ref, tokens_ref, routes_ref, gain_ref, router_ref, sems = refs
    copies = [
        pltpu.make_async_copy(tokens_hbm, tokens_ref, sems.at[0]),
        pltpu.make_async_copy(gain_hbm, gain_ref, sems.at[1]),
        pltpu.make_async_copy(routes_hbm, routes_ref, sems.at[2]),
        pltpu.make_async_copy(router_hbm, router_ref, sems.at[3]),
    ]
    for copy in copies:
        copy.start()
    heads = [
        pltpu.make_async_copy(gate_hbm.at[:, :head], gate_ref.at[:, :head], sems.at[4]),
        pltpu.make_async_copy(up_hbm.at[:, :head], up_ref.at[:, :head], sems.at[5]),
    ]
    for copy in heads:
        copy.start()
    for copy in copies:
        copy.wait()
    rows = tokens_ref.shape[0]
    experts = router_ref.shape[0]
    capacity = out_refs[0].shape[0]
    here = lax.axis_index("expert")

    def ordered(shape):
        place, labels = iota(shape, 0), jnp.zeros(shape, jnp.int32)
        for at, move in enumerate(moves):
            labels = jnp.where(place == at, target(here, move), labels)
        return labels

    widened = tokens_ref[...].astype(f32)
    inverse = lax.rsqrt(jnp.mean(widened * widened, axis=-1, keepdims=True) + norm_eps)
    normed = (widened * inverse * gain_ref[...]).astype(bf16)
    labels = ordered((experts, rows))
    hit = (routes_ref[0:1, :] == labels) | (routes_ref[1:2, :] == labels)
    hits = jnp.where(hit, 1.0, 0.0).astype(bf16)
    down, across = iota((rows, rows), 0), iota((rows, rows), 1)
    ranks = dot(hits, jnp.where(down < across, 1.0, 0.0).astype(bf16))
    ranks = jnp.where(hit, ranks, -1.0)
    places = iota((capacity, rows), 0).astype(f32)
    for e in range(experts):
        chosen = jnp.where(places == ranks[e : e + 1, :], 1.0, 0.0).astype(bf16)
        out_refs[e][...] = dot(chosen, normed).astype(bf16)
    hits_down = dot_nt(jnp.where(down == across, 1.0, 0.0).astype(bf16), hits)
    ranks_down = dot_nt(jnp.where(across < down, 1.0, 0.0).astype(bf16), hits)
    picks = ordered((experts, experts)) == iota((experts, experts), 1)
    router = dot(jnp.where(picks, 1.0, 0.0).astype(bf16), router_ref[...]).astype(bf16)
    logits = dot_nt(normed, router)
    both = jnp.sum(hits_down * logits, axis=-1, keepdims=True)
    slots_ref[...] = jnp.where(hits_down > 0.5, ranks_down, -1.0)
    weights_ref[...] = hits_down / (1.0 + jnp.exp(both - 2.0 * logits))
    for copy in heads:
        copy.wait()


def stack(x_refs, x_ref):
    rows = x_refs[0].shape[0]
    for at, ref in enumerate(x_refs):
        x_ref[at * rows : (at + 1) * rows, :] = ref[...]


def unstack(x, out_refs):
    rows = out_refs[0].shape[0]
    for at, ref in enumerate(out_refs):
        ref[...] = x[at * rows : (at + 1) * rows, :]


def hidden_block(x_ref, gate_ref, up_ref, hidden_ref, at):
    x = x_ref[...]
    gate_act = dot(x, gate_ref[:, at])
    up_act = dot(x, up_ref[:, at])
    hidden_ref[:, at] = (gate_act / (1.0 + jnp.exp(-gate_act)) * up_act).astype(bf16)


def first_expert_kernel(*refs, blocks, block, present, ahead):
    x_refs, out_refs = refs[:blocks], refs[blocks + 5 : 2 * blocks + 5]
    gate_hbm, up_hbm, down_hbm = refs[blocks : blocks + 3]
    gate_ref, up_ref, down_ref, x_ref, hidden_ref, sems = refs[2 * blocks + 5 :]
    steps = hidden_ref.shape[1] // block

    def part(step):
        return pl.ds(pl.multiple_of(step * block, block), block)

    def fetches(step):
        at = part(step)
        return (
            pltpu.make_async_copy(gate_hbm.at[:, at], gate_ref.at[:, at], sems.at[0, step]),
            pltpu.make_async_copy(up_hbm.at[:, at], up_ref.at[:, at], sems.at[1, step]),
        )

    down_fetch = pltpu.make_async_copy(down_hbm, down_ref, sems.at[2, 0])
    for step in range(present, ahead):
        for copy in fetches(step):
            copy.start()
    stack(x_refs, x_ref)

    def columns(step, carry):
        @pl.when(step + ahead < steps)
        def _():
            for copy in fetches(step + ahead):
                copy.start()

        @pl.when(step + ahead == steps)
        def _():
            down_fetch.start()

        @pl.when(step >= present)
        def _():
            for copy in fetches(step):
                copy.wait()

        hidden_block(x_ref, gate_ref, up_ref, hidden_ref, part(step))
        return carry

    lax.fori_loop(0, steps, columns, 0)
    down_fetch.wait()
    unstack(dot(hidden_ref[...], down_ref[...]).astype(bf16), out_refs)


def later_expert_kernel(*refs, blocks, block):
    x_refs, out_refs = refs[:blocks], refs[blocks + 3 : 2 * blocks + 3]
    gate_ref, up_ref, down_ref = refs[blocks : blocks + 3]
    x_ref, hidden_ref = refs[2 * blocks + 3 :]
    stack(x_refs, x_ref)

    def columns(step, carry):
        at = pl.ds(pl.multiple_of(step * block, block), block)
        hidden_block(x_ref, gate_ref, up_ref, hidden_ref, at)
        return carry

    lax.fori_loop(0, hidden_ref.shape[1] // block, columns, 0)
    unstack(dot(hidden_ref[...], down_ref[...]).astype(bf16), out_refs)


def expert_rows(xs, weights, heads, ahead=2):
    rows, width = xs[0].shape
    hidden = weights[0].shape[1]
    blocks = len(xs)
    places = range(blocks, blocks + 3)
    results = [jax.ShapeDtypeStruct(x.shape, bf16) for x in xs]
    scratch = [pltpu.VMEM((blocks * rows, width), bf16), pltpu.VMEM((blocks * rows, hidden), bf16)]
    if heads:
        out = call(
            functools.partial(
                first_expert_kernel, blocks=blocks, block=block, present=head // block, ahead=ahead
            ),
            results + [jax.ShapeDtypeStruct(w.shape, bf16) for w in weights],
            *xs, *weights, *heads,
            budget=20,
            outside=places,
            inside=range(blocks + 3, blocks + 5),
            input_output_aliases={blocks + 3: blocks, blocks + 4: blocks + 1},
            scratch_shapes=scratch + [pltpu.SemaphoreType.DMA((3, hidden // block))],
        )
        return out[:blocks], out[blocks:]
    out = call(
        functools.partial(later_expert_kernel, blocks=blocks, block=block),
        results,
        *xs, *weights,
        budget=16,
        inside=places,
        scratch_shapes=scratch,
    )
    return out, weights


def weighted_rows(slots_ref, weights_ref, back_refs, start):
    shape = slots_ref.shape[0], back_refs[0].shape[0]
    lanes = iota(shape, 1).astype(f32)
    terms = [
        jnp.where(lanes == slots_ref[:, e : e + 1], weights_ref[:, e : e + 1], 0.0)
        for e in range(start, start + len(back_refs))
    ]
    high, low = split(jnp.concatenate(terms, axis=1))
    back = jnp.concatenate([ref[...] for ref in back_refs], axis=0)
    return dot(high, back) + dot(low, back)


def early_combine_kernel(tokens_ref, slots_ref, weights_ref, *refs):
    *back_refs, mixed_ref = refs
    mixed_ref[...] = tokens_ref[...].astype(f32) + weighted_rows(slots_ref, weights_ref, back_refs, 0)


def combine_kernel(early_ref, slots_ref, weights_ref, lengths_ref, *refs):
    *back_refs, mixed_ref, embedded_ref, rounded_ref = refs
    rows = early_ref.shape[0]
    start = slots_ref.shape[1] - len(back_refs)
    mixed = early_ref[...] + weighted_rows(slots_ref, weights_ref, back_refs, start)
    mixed_ref[...] = mixed
    count = lengths_ref.shape[1]
    spans = jnp.broadcast_to(lengths_ref[...], (count, count)).astype(f32)
    down, across = iota((count, count), 0), iota((count, count), 1)
    ends = jnp.sum(jnp.where(across <= down, spans, 0.0), axis=1, keepdims=True)
    sizes = jnp.sum(jnp.where(across == down, spans, 0.0), axis=1, keepdims=True)
    places = iota((count, rows), 1).astype(f32)
    member = jnp.where((places >= ends - sizes) & (places < ends), 1.0, 0.0).astype(bf16)
    first, rest = split(mixed)
    second, third = split(mixed - first.astype(f32))
    pooled = (dot(member, first) + dot(member, second) + dot(member, third)) / sizes
    embedded = pooled * lax.rsqrt(jnp.sum(pooled * pooled, axis=-1, keepdims=True) + pool_eps)
    embedded_ref[...] = embedded
    rounded_ref[...] = embedded.astype(bf16)


def exp_sums(docs_ref, queries_ref):
    scores = dot_nt(docs_ref[...], queries_ref[...])
    return jnp.sum(jnp.exp(logit_scale * scores), axis=0, keepdims=True)


def own_scores(embedded, docs_ref, queries_ref):
    stacked = jnp.concatenate(split(embedded), axis=0)
    count = embedded.shape[0] // 2
    return fold(dot_nt(stacked, docs_ref[...]))[:count], fold(dot_nt(stacked, queries_ref[...]))[count:]


def early_gradient_kernel(queries_ref, docs_ref, embedded_ref, _, sums_ref, rows_ref, cols_ref):
    sums_ref[...] = exp_sums(docs_ref, queries_ref)
    rows_ref[...], cols_ref[...] = own_scores(embedded_ref[...], docs_ref, queries_ref)


def gradient_kernel(
    queries_ref, docs_ref, more_queries_ref, more_docs_ref, embedded_ref, sums_ref, rows_ref, cols_ref,
    query_grad_ref, doc_grad_ref,
):
    rank = lax.axis_index("dp") // 2 * (lax.axis_size("expert") // plane) + lax.axis_index("expert") // plane
    embedded = embedded_ref[...]
    count = embedded.shape[0] // 2
    first = rank * count
    here = queries_ref.shape[0]
    total = 2 * here
    queries, documents = embedded[:count], embedded[count:]
    sums = sums_ref[...] + exp_sums(more_docs_ref, queries_ref)
    more_sums = exp_sums(docs_ref, more_queries_ref) + exp_sums(more_docs_ref, more_queries_ref)
    sums = jnp.concatenate([sums, more_sums], axis=1)
    more_rows, more_cols = own_scores(embedded, more_docs_ref, more_queries_ref)
    rows = jnp.concatenate([rows_ref[...], more_rows], axis=1)
    cols = jnp.concatenate([cols_ref[...], more_cols], axis=1)
    own = iota((count, total), 1) == first + iota((count, total), 0)
    pair = jnp.exp(logit_scale * jnp.sum(queries * documents, axis=-1, keepdims=True))
    rows = jnp.where(own, 0.0, jnp.exp(logit_scale * rows))
    cols = jnp.where(own, 0.0, jnp.exp(logit_scale * cols))
    row_sum = jnp.sum(rows, axis=-1, keepdims=True) + pair
    diagonal = pair / row_sum - 1.0
    likely = jnp.concatenate([rows / row_sum, cols / sums], axis=0)
    likely = jnp.concatenate(split(likely), axis=0)
    near, far = likely[:, :here], likely[:, here:]
    by_docs = fold(dot(near, docs_ref[...]) + dot(far, more_docs_ref[...]))[:count]
    by_queries = fold(dot(near, queries_ref[...]) + dot(far, more_queries_ref[...]))[count:]
    query_grad_ref[...] = logit_scale * (by_docs + diagonal * documents)
    doc_grad_ref[...] = logit_scale * (by_queries + diagonal * queries)


def route(tokens, routes, norm_gain, router_weight, gate, up):
    rows, width = tokens.shape
    experts = router_weight.shape[1]
    operands = (tokens, routes.T, norm_gain, router_weight.T, gate, up)
    return call(
        functools.partial(route_kernel, head=head),
        [
            *[jax.ShapeDtypeStruct((rows // 2, width), bf16) for _ in range(experts)],
            jax.ShapeDtypeStruct((rows, experts), f32),
            jax.ShapeDtypeStruct((rows, experts), f32),
            jax.ShapeDtypeStruct(gate.shape, bf16),
            jax.ShapeDtypeStruct(up.shape, bf16),
        ],
        *operands,
        outside=range(6),
        scratch_shapes=[pltpu.VMEM(x.shape, x.dtype) for x in operands[:4]]
        + [pltpu.SemaphoreType.DMA((len(operands),))],
    )


def combine(tokens, slots, weights, backs, lengths):
    count, width = lengths.shape[1], tokens.shape[1]
    early = len(backs) - len(move_groups[-1])
    mixed = call(
        early_combine_kernel,
        jax.ShapeDtypeStruct(tokens.shape, f32),
        tokens, slots, weights, *backs[:early],
    )
    return call(
        combine_kernel,
        [
            jax.ShapeDtypeStruct(tokens.shape, f32),
            jax.ShapeDtypeStruct((count, width), f32),
            jax.ShapeDtypeStruct((count, width), bf16),
        ],
        mixed, slots, weights, lengths, *backs[early:],
    )


def info_nce(queries, docs, more_queries, more_docs, embedded, after):
    count, here = embedded.shape[0] // 2, queries.shape[0]
    scores = jax.ShapeDtypeStruct((count, here), f32)
    early = call(
        early_gradient_kernel,
        [jax.ShapeDtypeStruct((1, here), f32), scores, scores],
        queries, docs, embedded, after,
    )
    out = jax.ShapeDtypeStruct((count, embedded.shape[1]), f32)
    return call(
        gradient_kernel, [out, out], queries, docs, more_queries, more_docs, embedded, *early
    )


def body(tokens, routes, lengths, norm_gain, router_weight, gate_weight, up_weight, down_weight):
    width = tokens.shape[1]
    experts = router_weight.shape[1]
    matrices = [gate_weight[0], up_weight[0], down_weight[0]]
    *outgoing, slots, weights, gate, up = route(
        tokens, routes, norm_gain, router_weight, *matrices[:2]
    )

    def pairs(move, back):
        places = [(e, target(e, move)) for e in range(experts)]
        return [(to, start) for start, to in places] if back else places

    def send(x, move, back=False):
        return x if move == (0, 0) else lax.ppermute(x, "expert", pairs(move, back))

    incoming = {move: send(x, move) for move, x in zip(moves, outgoing)}
    backs, heads = [], [gate, up]
    for group in move_groups:
        results, matrices = expert_rows([incoming[move] for move in group], matrices, heads)
        heads = []
        backs += [send(x, move, back=True) for move, x in zip(group, results)]
    mixed, embedded, rounded = combine(tokens, slots, weights, backs, lengths)

    groups = lax.axis_size("dp")
    swap = [(i, i ^ 1) for i in range(groups)]
    colours = [[] for _ in range(2 * plane)]
    for device in range(groups * experts):
        dp, expert = divmod(device, experts)
        colours[(expert + 2 * (dp // line)) % plane * 2 + dp % 2].append(device)
    copies = jnp.broadcast_to(rounded[None], (len(colours[0]),) + rounded.shape)
    own = lax.all_to_all(
        copies, ("dp", "expert"), split_axis=0, concat_axis=0, tiled=True, axis_index_groups=colours
    )
    blocks = [
        own,
        lax.ppermute(own, "expert", pairs((3, 0), False)),
        lax.ppermute(own, "dp", [(i, (i - line) % groups) for i in range(groups)]),
        lax.ppermute(own, "expert", pairs((1, 0), False)),
    ]
    more = [lax.ppermute(x, "dp", swap) for x in blocks]
    half = rounded.shape[0] // 2

    def apart(xs):
        return [
            jnp.concatenate([x[:, at : at + half] for x in xs]).reshape(-1, width) for at in (0, half)
        ]

    query_grad, doc_grad = info_nce(*apart(blocks), *apart(more), embedded, more[0])
    return (mixed.astype(bf16), query_grad, doc_grad)


def solution(mesh):
    placed = (
        P(("dp", "expert"), None),
        P(("dp", "expert"), None),
        P(("dp", "expert"), None),
        P(),
        P(),
        P("expert", None, None),
        P("expert", None, None),
        P("expert", None, None),
    )
    return jax.shard_map(
        body,
        mesh=mesh,
        in_specs=placed,
        out_specs=(P(("dp", "expert"), None), P(("dp", "expert"), None), P(("dp", "expert"), None)),
        check_vma=False,
    )
```
